512 devices in a mesh: dp: 32 (over x, z), mp: 16 (over y, core).
Axes of the slice: x: 4, y: 8, z: 8, core: 2. Of those that a mesh axis runs over, the one named last changes fastest.
Arguments:
- inputs: bfloat16 [32, 1024, 2560], P('dp', 'mp'), may hold values from -6 to 6
- out_grads: bfloat16 [32, 1024, 5120], P('dp', None, 'mp'), may hold values from -6 to 6
- counts: int32 [32, 1024], P('dp'), may hold values from 1 to 16
- residual: bfloat16 [32, 2560, 5120], P('dp', None, 'mp'), may hold values from -3 to 3
- q_start: float32 [5120, 32], P('mp'), may hold values from -6 to 6
Outputs:
- update: bfloat16 [2560, 5120], P('dp', 'mp')
- residual_next: bfloat16 [32, 2560, 5120], P('dp', None, 'mp')
- q_next: float32 [5120, 32], P('mp')
The draws below stay inside these ranges and needn't reach their ends.
All inputs are finite; a program needn't handle non-finite values.
Results may differ from the reference program's by a relative error of at most 0.0055.
Values may be sent and summed in bfloat16 or wider, within the bound.
A program may use at most 64 MiB of HBM per device.

```python
import math
import jax
import jax.numpy as jnp
from jax import lax

R = 2560
C = 5120
RANK = 32
TOK = 1024
DIVISOR = 8
REPLICAS = 32
N_DP = 32


def touch_ends(result, rng, low, high):
    longest = result.shape.index(max(result.shape))
    spots = []
    for shift in (0, 1):
        where = [jax.random.randint(jax.random.fold_in(rng, axis), (), 0, length) for axis, length in enumerate(result.shape)]
        where[longest] = (where[longest] + shift) % result.shape[longest]
        spots.append(tuple(where))
    return result.at[spots[0]].set(low).at[spots[1]].set(high)


def level_of(stream_key, extent, pieces, least, top_value):
    loudness, own = 1.0, jax.random.fold_in(stream_key, 6)
    for position, parts in pieces:
        draws = jnp.exp(jax.random.uniform(jax.random.fold_in(own, position), (parts,), jnp.float32, least / len(pieces), top_value / len(pieces)))
        loudness = loudness * jnp.repeat(draws, extent[position] // parts).reshape([-1 if axis == position else 1 for axis in range(len(extent))])
    return loudness


def noise(rng, extent, spread, bound, split=(), dtype=jnp.bfloat16):
    entries = jax.random.normal(rng, extent, jnp.float32) * spread
    if len(split) > 0:
        entries = level_of(rng, extent, split, -0.22, 0.18) * entries
    return jnp.clip(entries, min=-bound, max=bound).astype(dtype)


def setup_inputs(seed: int = 0) -> dict:
    arg_keys = jax.random.split(jax.random.key(seed), 6)
    inputs = noise(arg_keys[0], (REPLICAS, TOK, R), 1.0, 6.0, ((0, 32), (1, 16)))
    out_grads = noise(arg_keys[1], (REPLICAS, TOK, C), 1.0, 6.0, ((0, 32), (2, 16)))
    counts = touch_ends(jax.random.randint(arg_keys[2], (REPLICAS, TOK), 1, 17), jax.random.fold_in(arg_keys[2], 1), 1, 16).astype(jnp.int32)
    residual = noise(arg_keys[3], (REPLICAS, R, C), 0.5, 3.0, ((0, 32), (2, 16)))
    q_start = noise(arg_keys[4], (C, RANK), 1.0, 6.0, ((0, 16),), jnp.float32)
    return {"inputs": inputs, "out_grads": out_grads, "counts": counts, "residual": residual, "q_start": q_start}


def reference(inputs, out_grads, counts, residual, q_start):
    scaling = 1.0 / math.sqrt(TOK)

    def one_replica(operands):
        acts, grads_out, weights_int = operands
        weighted = (grads_out.astype(jnp.float32) * (weights_int.astype(jnp.float32) / DIVISOR)[:, None]).astype(jnp.bfloat16)
        gradient = lax.dot_general(acts.astype(jnp.float32), weighted.astype(jnp.float32), (((0,), (0,)), ((), ())), preferred_element_type=jnp.float32)
        return gradient * scaling
    gradient = lax.map(one_replica, (inputs, out_grads, counts))
    merged = gradient + residual.astype(jnp.float32)
    p_sum = jnp.einsum('nrc,ck->rk', merged, q_start, precision=lax.Precision.HIGHEST)
    gram_matrix = jnp.dot(p_sum.T, p_sum, precision=lax.Precision.HIGHEST)
    factor = jnp.linalg.cholesky(gram_matrix)
    p_hat = lax.linalg.triangular_solve(factor, p_sum, left_side=False, lower=True, transpose_a=True)
    q_next = jnp.einsum('nrc,rk->ck', merged, p_hat, precision=lax.Precision.HIGHEST)
    approx = jnp.dot(p_hat, q_next.T, precision=lax.Precision.HIGHEST)
    update = approx.astype(jnp.bfloat16)
    residual_next = (merged - approx[None] / N_DP).astype(jnp.bfloat16)
    return (update, residual_next, q_next)
```

```python
import functools

import jax
import jax.numpy as jnp
from jax import lax
from jax.experimental import pallas as pl
from jax.experimental.pallas import tpu as pltpu
from jax.sharding import PartitionSpec as P

MESH = pl.DeviceIdType.MESH
F32, BF16 = jnp.float32, jnp.bfloat16
NX, NY, NZ, NC = 4, 8, 8, 2
ROWS, COLS, RANK, TOK = 2560, 320, 32, 1024
HALF = RANK // NC
BLOCK = TOK // (NY * NC)
PAIR = BLOCK * NC
XL = ROWS // NX
ZR = HALF // NZ
QR = RANK // NX
QL = 384
SUB = BLOCK // 2
SCALE = 1.0 / 32.0
DIVISOR = 8.0
NT = (((1,), (1,)), ((), ()))
NN = (((1,), (0,)), ((), ()))
TN = (((0,), (0,)), ((), ()))


def dot(a, b, dims):
    return lax.dot_general(a, b, dims, preferred_element_type=F32)


def dot_exact(a, b, dims):
    return lax.dot_general(a, b, dims, precision=lax.Precision.HIGHEST, preferred_element_type=F32)


def split3(v):
    high = v.astype(BF16)
    rest = v - high.astype(F32)
    mid = rest.astype(BF16)
    low = (rest - mid.astype(F32)).astype(BF16)
    return jnp.concatenate([high, mid, low], axis=0)


def sum3(v):
    n = v.shape[0] // 3
    return v[:n] + (v[n : 2 * n] + v[2 * n :])


def inverse_factor(gram):
    rows = lax.broadcasted_iota(jnp.int32, (RANK, 128), 0)
    lanes = lax.broadcasted_iota(jnp.int32, (RANK, 128), 1)
    eye = jnp.where(lanes == rows + RANK, 1.0, 0.0)
    work = jnp.concatenate([gram, jnp.zeros((RANK, 128 - RANK), F32)], axis=1) + eye

    def step(j, m):
        row = jnp.sum(jnp.where(rows == j, m, 0.0), axis=0, keepdims=True)
        col = jnp.sum(jnp.where(lanes == j, m, 0.0), axis=1, keepdims=True)
        pivot = jnp.sum(jnp.where(lanes[:1] == j, row, 0.0), axis=1, keepdims=True)
        inv = 1.0 / jnp.sqrt(pivot)
        row = row * inv
        return jnp.where(rows > j, m - (col * inv) * row, jnp.where(rows == j, row, m))

    return lax.fori_loop(0, RANK, step, work)[:, RANK : 2 * RANK]


def chain_kernel(
    inp_hbm, og_hbm, cnt_hbm, res_hbm, q_hbm,
    merged_hbm, phat_ref, qnext_ref,
    gbuf, og, cnt, res, q, wbuf, merged,
    wq, wqin, wqh, wqr, rq, rqin, ph, xr, p1, zs, zr, yr, zg, pa, pt,
    qb, qxr, qzr, qt,
    lsem, gsend, grecv, csend, crecv, cown, esend, erecv,
    wsend, wrecv, xsend, xrecv, zsend, zrecv, ysend, yrecv,
    zgsend, zgrecv, xgsend, xgrecv, qxsend, qxrecv, qzsend, qzrecv, qgsend, qgrecv,
):
    dp, mp = lax.axis_index("dp"), lax.axis_index("mp")
    x, z = dp // NZ, lax.rem(dp, NZ)
    y, c = mp // NC, lax.rem(mp, NC)

    def at_x(i):
        return (i * NZ + z, mp)

    def at_z(i):
        return (x * NZ + i, mp)

    def at_y(i):
        return (dp, i * NC + c)

    sibling = (dp, y * NC + (1 - c))

    def other(i, d, n):
        return lax.rem(i + d, n)

    def copy(src, dst, s, r, to):
        return pltpu.make_async_remote_copy(src, dst, s, r, device_id=to, device_id_type=MESH)

    loads = [
        pltpu.make_async_copy(og_hbm, og, lsem.at[0]),
        pltpu.make_async_copy(cnt_hbm, cnt, lsem.at[1]),
        pltpu.make_async_copy(q_hbm, q, lsem.at[2]),
        pltpu.make_async_copy(inp_hbm, gbuf.at[mp], lsem.at[3]),
        pltpu.make_async_copy(res_hbm, res, lsem.at[4]),
    ]
    for load in loads:
        load.start()

    barrier = pltpu.get_barrier_semaphore()
    peers = [sibling]
    peers += [at_x(other(x, d, NX)) for d in range(1, NX)]
    peers += [at_z(other(z, d, NZ)) for d in range(1, NZ)]
    peers += [at_y(other(y, d, NY)) for d in range(1, NY)]
    for peer in peers:
        pl.semaphore_signal(barrier, inc=1, device_id=peer, device_id_type=MESH)

    loads[0].wait()
    loads[1].wait()
    loads[2].wait()
    weight = jnp.broadcast_to(cnt[...].astype(F32) / DIVISOR, (8, TOK)).T[:, 0:1]
    wbuf[...] = (og[...].astype(F32) * weight).astype(BF16)
    q3 = split3(q[...].T)
    wq[...] = sum3(dot(q3, wbuf[...], NT)).reshape(NC, HALF, TOK)
    pl.semaphore_wait(barrier, len(peers))

    pending = []

    def go(cp):
        cp.start()
        pending.append(cp)
        return cp

    w_ex = go(copy(wq.at[1 - c], wqin, esend.at[0], erecv.at[0], sibling))
    loads[3].wait()
    own_ex = go(copy(gbuf.at[mp], gbuf.at[mp], esend.at[1], cown, sibling))
    w_ex.wait_recv()
    wqh[...] = wq[c] + wqin[...]
    for d in range(1, NY):
        i = other(y, d, NY)
        go(copy(wqh.at[:, pl.ds(pl.multiple_of(i * PAIR, PAIR), PAIR)], wqr.at[y], wsend.at[d], wrecv.at[y], at_y(i)))

    def ring_block(up, h):
        return lax.rem(y + (NY - h if up else h), NY) * NC + c

    def ring_send(up, h, s):
        part = gbuf.at[ring_block(up, h), pl.ds(s * SUB, SUB)]
        to = at_y(other(y, 1 if up else NY - 1, NY))
        u = 0 if up else 1
        go(copy(part, part, gsend.at[u, h, s], grecv.at[u, h, s], to))

    def ring_recv(up, h, s):
        part = gbuf.at[ring_block(up, h), pl.ds(s * SUB, SUB)]
        u = 0 if up else 1
        copy(part, part, gsend.at[u, h - 1, s], grecv.at[u, h - 1, s], sibling).wait_recv()
        go(copy(part, part, csend.at[u, h - 1, s], crecv.at[u, h - 1, s], sibling))

    def ring_step(h, s):
        for up in (True, False):
            if h == NY // 2 and (s == 0) != up:
                continue
            ring_recv(up, h, s)
            if h < NY // 2 - 1 or (h == NY // 2 - 1 and (s == 0) == up):
                ring_send(up, h, s)

    for s in range(2):
        ring_send(True, 0, s)
        ring_send(False, 0, s)

    loads[4].wait()
    rq[...] = sum3(dot(q3, res[...], NT)).reshape(NC, HALF, ROWS)
    r_ex = go(copy(rq.at[1 - c], rqin, esend.at[2], erecv.at[1], sibling))
    wqr[y] = wqh[:, pl.ds(pl.multiple_of(y * PAIR, PAIR), PAIR)]
    for d in range(1, NY):
        i = other(y, d, NY)
        copy(wqr.at[i], wqr.at[i], wsend.at[d], wrecv.at[i], sibling).wait_recv()
    w_tok = wqr[0]
    for i in range(1, NY):
        w_tok = w_tok + wqr[i]
    sib_slot = gbuf.at[y * NC + (1 - c)]
    copy(sib_slot, sib_slot, esend.at[1], cown, sibling).wait_recv()
    pair = gbuf[pl.ds(y * NC, NC)].reshape(PAIR, ROWS)
    p_tok = sum3(dot(split3(w_tok * SCALE), pair, NN))
    r_ex.wait_recv()
    ph[...] = p_tok + (rq[c] + rqin[...])

    for d in range(1, NX):
        i = other(x, d, NX)
        go(copy(ph.at[:, pl.ds(pl.multiple_of(i * XL, 128), XL)], xr.at[x], xsend.at[d], xrecv.at[x], at_x(i)))
    ring_step(1, 0)
    ring_step(1, 1)
    xr[x] = ph[:, pl.ds(pl.multiple_of(x * XL, 128), XL)]
    for d in range(1, NX):
        i = other(x, d, NX)
        copy(xr.at[i], xr.at[i], xsend.at[d], xrecv.at[i], sibling).wait_recv()
    total = xr[0]
    for i in range(1, NX):
        total = total + xr[i]
    for i in range(NZ):
        zs[i] = total[ZR * i : ZR * (i + 1)]
    for d in range(1, NZ):
        i = other(z, d, NZ)
        go(copy(zs.at[i], zr.at[z], zsend.at[d], zrecv.at[z], at_z(i)))
    ring_step(2, 0)
    zr[z] = zs[z]
    for d in range(1, NZ):
        i = other(z, d, NZ)
        copy(zr.at[i], zr.at[i], zsend.at[d], zrecv.at[i], sibling).wait_recv()
    total = zr[0]
    for i in range(1, NZ):
        total = total + zr[i]
    yr[y] = total
    for d in range(1, NY):
        i = other(y, d, NY)
        go(copy(yr.at[y], yr.at[y], ysend.at[d], yrecv.at[y], at_y(i)))
    ring_step(2, 1)
    for d in range(1, NY):
        i = other(y, d, NY)
        copy(yr.at[i], yr.at[i], ysend.at[d], yrecv.at[i], sibling).wait_recv()
    total = yr[0]
    for i in range(1, NY):
        total = total + yr[i]
    zg[z] = total
    for d in range(1, NZ):
        i = other(z, d, NZ)
        go(copy(zg.at[z], zg.at[z], zgsend.at[d], zgrecv.at[z], at_z(i)))
    ring_step(3, 0)
    ring_step(3, 1)
    for d in range(1, NZ):
        i = other(z, d, NZ)
        copy(zg.at[i], zg.at[i], zgsend.at[d], zgrecv.at[i], sibling).wait_recv()
    for i in range(NZ):
        pa[ZR * i : ZR * (i + 1), :] = zg[i]
    mine = pl.ds(pl.multiple_of(x * XL, 128), XL)
    for d in range(1, NX):
        i = other(x, d, NX)
        go(copy(pa, pt.at[c, :, mine], xgsend.at[d], xgrecv.at[x], at_x(i)))
    pt[c, :, mine] = pa[...]
    for d in range(1, NX):
        i = other(x, d, NX)
        theirs = pt.at[c, :, pl.ds(pl.multiple_of(i * XL, 128), XL)]
        copy(theirs, theirs, xgsend.at[d], xgrecv.at[i], sibling).wait_recv()
    go(copy(pt.at[c], pt.at[c], esend.at[3], erecv.at[2], sibling))
    ring_step(4, 0)
    ring_step(4, 1)
    for h in range(1, NY // 2 + 1):
        for s in range(2):
            for up in (True, False):
                if h == NY // 2 and (s == 0) != up:
                    continue
                u = 0 if up else 1
                slot = lax.rem(y + (NY - h if up else h), NY) * NC + (1 - c)
                part = gbuf.at[slot, pl.ds(s * SUB, SUB)]
                copy(part, part, csend.at[u, h - 1, s], crecv.at[u, h - 1, s], sibling).wait_recv()
    copy(pt.at[1 - c], pt.at[1 - c], esend.at[3], erecv.at[2], sibling).wait_recv()

    p = pt[...].reshape(RANK, ROWS)
    p3 = split3(p)
    tokens = gbuf[...].reshape(TOK, ROWS)
    u3 = split3(sum3(dot(p3, tokens, NT)) * SCALE)
    q_part = sum3(dot(u3, wbuf[...], NN)) + sum3(dot(p3, res[...], NN))
    qb[...] = jnp.concatenate([q_part, jnp.zeros((RANK, QL - COLS), F32)], axis=1)
    for d in range(1, NX):
        i = other(x, d, NX)
        go(copy(qb.at[pl.ds(pl.multiple_of(i * QR, QR), QR)], qxr.at[x], qxsend.at[d], qxrecv.at[x], at_x(i)))

    step_cols = 512

    def grad(i, carry):
        at = pl.ds(pl.multiple_of(i * step_cols, step_cols), step_cols)
        g = dot(gbuf[:, :, at].reshape(TOK, step_cols), wbuf[...], TN)
        merged[at, :] = g * SCALE + res[at, :].astype(F32)
        return carry

    lax.fori_loop(0, ROWS // step_cols, grad, 0)
    store = pltpu.make_async_copy(merged, merged_hbm, lsem.at[5])
    store.start()
    qxr[x] = qb[pl.ds(pl.multiple_of(x * QR, QR), QR), :]
    for d in range(1, NX):
        i = other(x, d, NX)
        copy(qxr.at[i], qxr.at[i], qxsend.at[d], qxrecv.at[i], sibling).wait_recv()
    total = qxr[0]
    for i in range(1, NX):
        total = total + qxr[i]
    qzr[z] = total
    for d in range(1, NZ):
        i = other(z, d, NZ)
        go(copy(qzr.at[z], qzr.at[z], qzsend.at[d], qzrecv.at[z], at_z(i)))
    inv = inverse_factor(dot_exact(p, p, NT))
    phat_ref[...] = dot_exact(inv, p, NN)
    for d in range(1, NZ):
        i = other(z, d, NZ)
        copy(qzr.at[i], qzr.at[i], qzsend.at[d], qzrecv.at[i], sibling).wait_recv()
    total = qzr[0]
    for i in range(1, NZ):
        total = total + qzr[i]
    qt[x] = total
    for d in range(1, NX):
        i = other(x, d, NX)
        go(copy(qt.at[x], qt.at[x], qgsend.at[d], qgrecv.at[x], at_x(i)))
    for d in range(1, NX):
        i = other(x, d, NX)
        copy(qt.at[i], qt.at[i], qgsend.at[d], qgrecv.at[i], sibling).wait_recv()
    qnext_ref[...] = dot_exact(inv, qt[...].reshape(RANK, QL), NN)
    store.wait()
    for cp in pending:
        cp.wait_send()


def chain(inputs, out_grads, counts, residual, q_start):
    dma = pltpu.SemaphoreType.DMA
    vmem = pltpu.VMEM
    return pl.pallas_call(
        chain_kernel,
        out_shape=(
            jax.ShapeDtypeStruct((ROWS, COLS), F32),
            jax.ShapeDtypeStruct((RANK, ROWS), F32),
            jax.ShapeDtypeStruct((RANK, QL), F32),
        ),
        in_specs=[pl.BlockSpec(memory_space=pl.ANY)] * 5,
        out_specs=(
            pl.BlockSpec(memory_space=pl.ANY),
            pl.BlockSpec(memory_space=pltpu.VMEM),
            pl.BlockSpec(memory_space=pltpu.VMEM),
        ),
        scratch_shapes=[
            vmem((NY * NC, BLOCK, ROWS), BF16),
            vmem((TOK, COLS), BF16),
            vmem((1, TOK), jnp.int32),
            vmem((ROWS, COLS), BF16),
            vmem((COLS, RANK), F32),
            vmem((TOK, COLS), BF16),
            vmem((ROWS, COLS), F32),
            vmem((NC, HALF, TOK), F32),
            vmem((HALF, TOK), F32),
            vmem((HALF, TOK), F32),
            vmem((NY, HALF, PAIR), F32),
            vmem((NC, HALF, ROWS), F32),
            vmem((HALF, ROWS), F32),
            vmem((HALF, ROWS), F32),
            vmem((NX, HALF, XL), F32),
            vmem((HALF, XL), F32),
            vmem((NZ, ZR, XL), F32),
            vmem((NZ, ZR, XL), F32),
            vmem((NY, ZR, XL), F32),
            vmem((NZ, ZR, XL), F32),
            vmem((HALF, XL), F32),
            vmem((NC, HALF, ROWS), F32),
            vmem((RANK, QL), F32),
            vmem((NX, QR, QL), F32),
            vmem((NZ, QR, QL), F32),
            vmem((NX, QR, QL), F32),
            dma((6,)),
            dma((2, 4, 2)), dma((2, 4, 2)),
            dma((2, 4, 2)), dma((2, 4, 2)),
            dma,
            dma((4,)), dma((3,)),
            dma((NY,)), dma((NY,)),
            dma((NX,)), dma((NX,)),
            dma((NZ,)), dma((NZ,)),
            dma((NY,)), dma((NY,)),
            dma((NZ,)), dma((NZ,)),
            dma((NX,)), dma((NX,)),
            dma((NX,)), dma((NX,)),
            dma((NZ,)), dma((NZ,)),
            dma((NX,)), dma((NX,)),
        ],
        compiler_params=pltpu.CompilerParams(
            collective_id=0, has_side_effects=True, vmem_limit_bytes=48 << 20
        ),
        name="chain",
    )(inputs, out_grads, counts, residual, q_start)


FINAL_ROWS = 512


def final_kernel(merged_ref, phat_ref, qnext_ref, update_ref, res_ref, q_ref, approx):
    i = pl.program_id(0)

    def high_low(v):
        high = v.astype(BF16)
        return high, (v - high.astype(F32)).astype(BF16)

    p_high, p_low = high_low(phat_ref[...])
    q_high, q_low = high_low(qnext_ref[...][:, :COLS])
    block = dot(
        jnp.concatenate([p_high, p_high, p_low], axis=0),
        jnp.concatenate([q_high, q_low, q_high], axis=0),
        TN,
    )
    res_ref[...] = (merged_ref[...] - block * (1.0 / (NX * NZ))).astype(BF16)
    approx[pl.ds(pl.multiple_of(i * FINAL_ROWS, FINAL_ROWS), FINAL_ROWS), :] = block

    @pl.when(i == 0)
    def _():
        q_ref[...] = qnext_ref[...].T[:COLS]

    @pl.when(i == pl.num_programs(0) - 1)
    def _():
        n = ROWS // (NX * NZ)
        start = pl.multiple_of(lax.axis_index("dp") * n, 8)
        update_ref[...] = approx[pl.ds(start, n), :].astype(BF16)


def final(merged, phat, qnext):
    n = ROWS // (NX * NZ)
    return pl.pallas_call(
        final_kernel,
        grid=(ROWS // FINAL_ROWS,),
        out_shape=(
            jax.ShapeDtypeStruct((n, COLS), BF16),
            jax.ShapeDtypeStruct((ROWS, COLS), BF16),
            jax.ShapeDtypeStruct((COLS, RANK), F32),
        ),
        in_specs=[
            pl.BlockSpec((FINAL_ROWS, COLS), lambda i: (i, 0)),
            pl.BlockSpec((RANK, FINAL_ROWS), lambda i: (0, i)),
            pl.BlockSpec((RANK, QL), lambda i: (0, 0)),
        ],
        out_specs=(
            pl.BlockSpec((n, COLS), lambda i: (0, 0)),
            pl.BlockSpec((FINAL_ROWS, COLS), lambda i: (i, 0)),
            pl.BlockSpec((COLS, RANK), lambda i: (0, 0)),
        ),
        scratch_shapes=[pltpu.VMEM((ROWS, COLS), F32)],
        compiler_params=pltpu.CompilerParams(vmem_limit_bytes=32 << 20),
        name="final",
    )(merged, phat, qnext)


def local(inputs, out_grads, counts, residual, q_start):
    merged, phat, qnext = chain(inputs[0], out_grads[0], counts, residual[0], q_start)
    update, residual_next, q_next = final(merged, phat, qnext)
    return update, residual_next[None], q_next


def solution(mesh):
    return jax.shard_map(
        local,
        mesh=mesh,
        in_specs=(
            P("dp", "mp", None),
            P("dp", None, "mp"),
            P("dp", None),
            P("dp", None, "mp"),
            P("mp", None),
        ),
        out_specs=(P("dp", "mp"), P("dp", None, "mp"), P("mp", None)),
        check_vma=False,
    )
```

```python
import functools

import jax
import jax.numpy as jnp
from jax import lax
from jax.experimental import pallas as pl
from jax.experimental.pallas import tpu as pltpu
from jax.sharding import PartitionSpec as P

MESH = pl.DeviceIdType.MESH
F32, BF16 = jnp.float32, jnp.bfloat16
NX, NY, NZ, NC = 4, 8, 8, 2
ROWS, COLS, RANK, TOK = 2560, 320, 32, 1024
HALF = RANK // NC
BLOCK = TOK // (NY * NC)
PAIR = BLOCK * NC
XL = ROWS // NX
ZR = HALF // NZ
QR = RANK // NX
QL = 384
SUB = BLOCK // 2
GRAD_LANES = 640


def far_first(*sizes):
    offsets = [()]
    for n in sizes:
        offsets = [o + (d,) for o in offsets for d in range(n)]
    return sorted(offsets, key=lambda o: -sum(min(d, n - d) for d, n in zip(o, sizes)))[:-1]


FAR_X, FAR_Y, FAR_Z = ([d for (d,) in far_first(n)] for n in (NX, NY, NZ))
FAR_PLANE = far_first(NX, NZ)
SCALE = 1.0 / 32.0
DIVISOR = 8.0
NT = (((1,), (1,)), ((), ()))
NN = (((1,), (0,)), ((), ()))
TN = (((0,), (0,)), ((), ()))


def dot(a, b, dims):
    return lax.dot_general(a, b, dims, preferred_element_type=F32)


def dot_exact(a, b, dims):
    return lax.dot_general(a, b, dims, precision=lax.Precision.HIGHEST, preferred_element_type=F32)


def split3(v):
    high = v.astype(BF16)
    rest = v - high.astype(F32)
    mid = rest.astype(BF16)
    low = (rest - mid.astype(F32)).astype(BF16)
    return jnp.concatenate([high, mid, low], axis=0)


def sum3(v):
    n = v.shape[0] // 3
    return v[:n] + (v[n : 2 * n] + v[2 * n :])


def inverse_factor(gram):
    rows = lax.broadcasted_iota(jnp.int32, (RANK, 128), 0)
    lanes = lax.broadcasted_iota(jnp.int32, (RANK, 128), 1)
    eye = jnp.where(lanes == rows + RANK, 1.0, 0.0)
    work = jnp.concatenate([gram, jnp.zeros((RANK, 128 - RANK), F32)], axis=1) + eye

    pivots = jnp.ones((RANK, 128), F32)
    for j in range(RANK):
        col = jnp.broadcast_to(work[:, j : j + 1], (RANK, 128))
        pivot = col[j : j + 1]
        pivots = jnp.where(rows == j, pivot, pivots)
        work = jnp.where(rows > j, work - col * (work[j : j + 1] / pivot), work)
    return (work / jnp.sqrt(pivots))[:, RANK : 2 * RANK]


def chain_kernel(
    inp_hbm, og_hbm, cnt_hbm, res_hbm, q_hbm,
    merged, phat_ref, qnext_ref,
    gbuf, og, cnt, res, q, wbuf,
    wq, wqin, wqh, wqr, rq, rqin, ph, ps, pr, yr, pg, pt,
    qb, qxr, qzr, qt,
    lsem, gsend, grecv, csend, crecv, cown, esend, erecv,
    wsend, wrecv, psend, precv, ysend, yrecv, pgsend, pgrecv, plane, qxsend, qxrecv, qzsend, qzrecv, qgsend, qgrecv,
):
    dp, mp = lax.axis_index("dp"), lax.axis_index("mp")
    x, z = dp // NZ, lax.rem(dp, NZ)
    y, c = mp // NC, lax.rem(mp, NC)

    def at_x(i):
        return (i * NZ + z, mp)

    def at_z(i):
        return (x * NZ + i, mp)

    def at_y(i):
        return (dp, i * NC + c)

    sibling = (dp, y * NC + (1 - c))

    def other(i, d, n):
        return lax.rem(i + d, n)

    def at_dp(i):
        return (i, mp)

    def offset(dx, dz):
        return other(x, dx, NX) * NZ + other(z, dz, NZ)

    def copy(src, dst, s, r, to):
        return pltpu.make_async_remote_copy(src, dst, s, r, device_id=to, device_id_type=MESH)

    loads = [
        pltpu.make_async_copy(og_hbm, og, lsem.at[0]),
        pltpu.make_async_copy(cnt_hbm, cnt, lsem.at[1]),
        pltpu.make_async_copy(q_hbm, q, lsem.at[2]),
        pltpu.make_async_copy(inp_hbm, gbuf.at[mp], lsem.at[3]),
        pltpu.make_async_copy(res_hbm, res, lsem.at[4]),
    ]
    for load in loads:
        load.start()

    barrier = pltpu.get_barrier_semaphore()
    peers = [sibling]
    peers += [at_x(other(x, d, NX)) for d in range(1, NX)]
    peers += [at_z(other(z, d, NZ)) for d in range(1, NZ)]
    peers += [at_y(other(y, d, NY)) for d in range(1, NY)]
    for peer in peers:
        pl.semaphore_signal(barrier, inc=1, device_id=peer, device_id_type=MESH)

    loads[0].wait()
    loads[1].wait()
    loads[2].wait()
    weight = cnt[...].astype(F32) * (SCALE / DIVISOR)
    wbuf[...] = (og[...].astype(F32) * weight).astype(BF16)
    q3 = split3(q[...])
    wq[...] = sum3(dot(q3, wbuf[...], NN)).reshape(NC, HALF, TOK)
    pl.semaphore_wait(barrier, len(peers))
    for d in FAR_Z:
        pl.semaphore_signal(plane, inc=1, device_id=at_z(other(z, d, NZ)), device_id_type=MESH)

    pending = []

    def go(cp):
        cp.start()
        pending.append(cp)
        return cp

    w_ex = go(copy(wq.at[1 - c], wqin, esend.at[0], erecv.at[0], sibling))
    loads[3].wait()
    own_ex = go(copy(gbuf.at[mp], gbuf.at[mp], esend.at[1], cown, sibling))
    w_ex.wait_recv()
    wqh[...] = wq[c] + wqin[...]
    for d in FAR_Y:
        i = other(y, d, NY)
        go(copy(wqh.at[:, pl.ds(pl.multiple_of(i * PAIR, PAIR), PAIR)], wqr.at[y], wsend.at[d], wrecv.at[y], at_y(i)))

    def ring_block(up, h):
        return lax.rem(y + (NY - h if up else h), NY) * NC + c

    def ring_send(up, h, s):
        part = gbuf.at[ring_block(up, h), pl.ds(s * SUB, SUB)]
        to = at_y(other(y, 1 if up else NY - 1, NY))
        u = 0 if up else 1
        go(copy(part, part, gsend.at[u, h, s], grecv.at[u, h, s], to))

    def ring_recv(up, h, s):
        part = gbuf.at[ring_block(up, h), pl.ds(s * SUB, SUB)]
        u = 0 if up else 1
        copy(part, part, gsend.at[u, h - 1, s], grecv.at[u, h - 1, s], sibling).wait_recv()
        go(copy(part, part, csend.at[u, h - 1, s], crecv.at[u, h - 1, s], sibling))

    def ring_step(h, s):
        for up in (True, False):
            if h == NY // 2 and (s == 0) != up:
                continue
            ring_recv(up, h, s)
            if h < NY // 2 - 1 or (h == NY // 2 - 1 and (s == 0) == up):
                ring_send(up, h, s)

    def ring_sibling(h):
        for s in range(2):
            for up in (True, False):
                if h == NY // 2 and (s == 0) != up:
                    continue
                u = 0 if up else 1
                slot = lax.rem(y + (NY - h if up else h), NY) * NC + (1 - c)
                part = gbuf.at[slot, pl.ds(s * SUB, SUB)]
                copy(part, part, csend.at[u, h - 1, s], crecv.at[u, h - 1, s], sibling).wait_recv()

    def grad(up, down, first=False):
        up, down = lax.rem(y + NY - up, NY), lax.rem(y + down, NY)

        def lanes(i):
            return pl.ds(pl.multiple_of(i * PAIR, PAIR), PAIR)

        w = jnp.concatenate([wbuf[:, lanes(up)], wbuf[:, lanes(down)]], axis=1)

        def step(i, carry):
            at = pl.ds(pl.multiple_of(i * GRAD_LANES, GRAD_LANES), GRAD_LANES)
            t = jnp.concatenate(
                [gbuf[pl.ds(k * NC, NC), :, at].reshape(PAIR, GRAD_LANES) for k in (up, down)], axis=0
            )
            base = res[:, at].astype(F32) if first else merged[:, at]
            merged[:, at] = base + dot(w, t, NN)
            return carry

        lax.fori_loop(0, ROWS // GRAD_LANES, step, 0)

    for s in range(2):
        ring_send(True, 0, s)
        ring_send(False, 0, s)

    loads[4].wait()
    rq[...] = sum3(dot(q3, res[...], NN)).reshape(NC, HALF, ROWS)
    r_ex = go(copy(rq.at[1 - c], rqin, esend.at[2], erecv.at[1], sibling))
    wqr[y] = wqh[:, pl.ds(pl.multiple_of(y * PAIR, PAIR), PAIR)]
    for d in range(1, NY):
        i = other(y, d, NY)
        copy(wqr.at[i], wqr.at[i], wsend.at[d], wrecv.at[i], sibling).wait_recv()
    w_tok = wqr[0]
    for i in range(1, NY):
        w_tok = w_tok + wqr[i]
    sib_slot = gbuf.at[y * NC + (1 - c)]
    copy(sib_slot, sib_slot, esend.at[1], cown, sibling).wait_recv()
    pair = gbuf[pl.ds(y * NC, NC)].reshape(PAIR, ROWS)
    p_tok = sum3(dot(split3(w_tok), pair, NN))
    r_ex.wait_recv()
    ph[...] = p_tok + (rq[c] + rqin[...])

    for i in range(NX):
        for k in range(NZ):
            ps[i * NZ + k] = ph[ZR * k : ZR * (k + 1), XL * i : XL * (i + 1)]
    pl.semaphore_wait(plane, NZ - 1)
    for n, (dx, dz) in enumerate(FAR_PLANE):
        i = offset(dx, dz)
        go(copy(ps.at[i], pr.at[dp], psend.at[n], precv.at[dp], at_dp(i)))
    ring_step(1, 0)
    ring_step(1, 1)
    pr[dp] = ps[dp]
    for dx, dz in FAR_PLANE[::-1]:
        i = offset(dx, dz)
        copy(pr.at[i], pr.at[i], psend.at[0], precv.at[i], sibling).wait_recv()
    yr[y] = jnp.sum(pr[...], axis=0)
    for d in FAR_Y:
        i = other(y, d, NY)
        go(copy(yr.at[y], yr.at[y], ysend.at[d], yrecv.at[y], at_y(i)))
    ring_step(2, 0)
    ring_step(2, 1)
    ring_sibling(1)
    grad(1, 1, first=True)
    for d in range(1, NY):
        i = other(y, d, NY)
        copy(yr.at[i], yr.at[i], ysend.at[d], yrecv.at[i], sibling).wait_recv()
    pg[dp] = jnp.sum(yr[...], axis=0)
    for n, (dx, dz) in enumerate(FAR_PLANE):
        i = offset(dx, dz)
        go(copy(pg.at[dp], pg.at[dp], pgsend.at[n], pgrecv.at[dp], at_dp(i)))
    ring_step(3, 0)
    ring_step(3, 1)
    ring_sibling(2)
    grad(2, 2)
    for dx, dz in FAR_PLANE[::-1]:
        i = offset(dx, dz)
        copy(pg.at[i], pg.at[i], pgsend.at[0], pgrecv.at[i], sibling).wait_recv()
    for i in range(NX):
        for k in range(NZ):
            pt[c, ZR * k : ZR * (k + 1), XL * i : XL * (i + 1)] = pg[i * NZ + k]
    go(copy(pt.at[c], pt.at[c], esend.at[3], erecv.at[2], sibling))
    ring_step(4, 0)
    ring_step(4, 1)
    ring_sibling(3)
    ring_sibling(4)
    copy(pt.at[1 - c], pt.at[1 - c], esend.at[3], erecv.at[2], sibling).wait_recv()

    p = pt[...].reshape(RANK, ROWS)
    p3 = split3(p)
    tokens = gbuf[...].reshape(TOK, ROWS)
    u3 = split3(sum3(dot(p3, tokens, NT)))
    q_part = sum3(dot(u3, wbuf[...], NT)) + sum3(dot(p3, res[...], NT))
    qb[...] = jnp.concatenate([q_part, jnp.zeros((RANK, QL - COLS), F32)], axis=1)
    for d in FAR_X:
        i = other(x, d, NX)
        go(copy(qb.at[pl.ds(pl.multiple_of(i * QR, QR), QR)], qxr.at[x], qxsend.at[d], qxrecv.at[x], at_x(i)))

    grad(3, 3)
    grad(0, 4)
    qxr[x] = qb[pl.ds(pl.multiple_of(x * QR, QR), QR), :]
    for d in range(1, NX):
        i = other(x, d, NX)
        copy(qxr.at[i], qxr.at[i], qxsend.at[d], qxrecv.at[i], sibling).wait_recv()
    total = qxr[0]
    for i in range(1, NX):
        total = total + qxr[i]
    qzr[z] = total
    for d in FAR_Z:
        i = other(z, d, NZ)
        go(copy(qzr.at[z], qzr.at[z], qzsend.at[d], qzrecv.at[z], at_z(i)))
    inv = inverse_factor(dot_exact(p, p, NT))
    for d in range(1, NZ):
        i = other(z, d, NZ)
        copy(qzr.at[i], qzr.at[i], qzsend.at[d], qzrecv.at[i], sibling).wait_recv()
    total = qzr[0]
    for i in range(1, NZ):
        total = total + qzr[i]
    qt[x] = total
    for d in FAR_X:
        i = other(x, d, NX)
        go(copy(qt.at[x], qt.at[x], qgsend.at[d], qgrecv.at[x], at_x(i)))
    phat_ref[...] = dot_exact(inv, p, NN)
    for d in range(1, NX):
        i = other(x, d, NX)
        copy(qt.at[i], qt.at[i], qgsend.at[d], qgrecv.at[i], sibling).wait_recv()
    qnext_ref[...] = dot_exact(inv, qt[...].reshape(RANK, QL), NN)
    for cp in pending:
        cp.wait_send()


def chain(inputs, out_grads, counts, residual, q_start):
    dma = pltpu.SemaphoreType.DMA
    vmem = pltpu.VMEM
    return pl.pallas_call(
        chain_kernel,
        out_shape=(
            vmem((COLS, ROWS), F32),
            vmem((RANK, ROWS), F32),
            vmem((RANK, QL), F32),
        ),
        in_specs=[pl.BlockSpec(memory_space=pl.ANY)] * 5,
        out_specs=(
            pl.BlockSpec(memory_space=pltpu.VMEM),
            pl.BlockSpec(memory_space=pltpu.VMEM),
            pl.BlockSpec(memory_space=pltpu.VMEM),
        ),
        scratch_shapes=[
            vmem((NY * NC, BLOCK, ROWS), BF16),
            vmem((COLS, TOK), BF16),
            vmem((1, TOK), jnp.int32),
            vmem((COLS, ROWS), BF16),
            vmem((RANK, COLS), F32),
            vmem((COLS, TOK), BF16),
            vmem((NC, HALF, TOK), F32),
            vmem((HALF, TOK), F32),
            vmem((HALF, TOK), F32),
            vmem((NY, HALF, PAIR), F32),
            vmem((NC, HALF, ROWS), F32),
            vmem((HALF, ROWS), F32),
            vmem((HALF, ROWS), F32),
            vmem((NX * NZ, ZR, XL), F32),
            vmem((NX * NZ, ZR, XL), F32),
            vmem((NY, ZR, XL), F32),
            vmem((NX * NZ, ZR, XL), F32),
            vmem((NC, HALF, ROWS), F32),
            vmem((RANK, QL), F32),
            vmem((NX, QR, QL), F32),
            vmem((NZ, QR, QL), F32),
            vmem((NX, QR, QL), F32),
            dma((5,)),
            dma((2, 4, 2)), dma((2, 4, 2)),
            dma((2, 4, 2)), dma((2, 4, 2)),
            dma,
            dma((4,)), dma((3,)),
            dma((NY,)), dma((NY,)),
            dma((NX * NZ,)), dma((NX * NZ,)),
            dma((NY,)), dma((NY,)),
            dma((NX * NZ,)), dma((NX * NZ,)),
            pltpu.SemaphoreType.REGULAR,
            dma((NX,)), dma((NX,)),
            dma((NZ,)), dma((NZ,)),
            dma((NX,)), dma((NX,)),
        ],
        compiler_params=pltpu.CompilerParams(
            collective_id=0, has_side_effects=True, vmem_limit_bytes=40 << 20
        ),
        name="chain",
    )(*(pltpu.with_memory_space_constraint(a, pltpu.HBM) for a in (inputs, out_grads, counts, residual, q_start)))


FINAL_LANES = 640
OWN = ROWS // (NX * NZ)


def final_kernel(
    merged_ref, phat_ref, qnext_ref, update_hbm, res_hbm, q_hbm,
    update, res, q, turned, sems,
):
    def high_low(v):
        high = v.astype(BF16)
        return high, (v - high.astype(F32)).astype(BF16)

    stores = []

    def store(src, dst):
        stores.append(pltpu.make_async_copy(src, dst, sems.at[len(stores)]))
        stores[-1].start()

    q[...] = qnext_ref[:, :COLS]
    store(q, q_hbm)
    high, low = high_low(qnext_ref[...].T)
    q_cols = jnp.concatenate([high, low, high], axis=1)[:COLS]
    for i in range(ROWS // FINAL_LANES):
        at = slice(i * FINAL_LANES, (i + 1) * FINAL_LANES)
        high, low = high_low(phat_ref[:, at])
        block = dot(q_cols, jnp.concatenate([high, high, low], axis=0), NN)
        res[:, at] = (merged_ref[:, at] - block * (1.0 / (NX * NZ))).astype(BF16)
        store(res.at[:, at], res_hbm.at[:, at])
    first = lax.axis_index("dp") * OWN
    base = jnp.minimum(first // 128, ROWS // 128 - 2) * 128
    turned[...] = phat_ref[:, pl.ds(pl.multiple_of(base, 128), 256)].T
    high, low = high_low(turned[pl.ds(pl.multiple_of(first - base, 8), OWN), :])
    update[...] = dot(jnp.concatenate([high, high, low], axis=1), q_cols, NT).astype(BF16)
    store(update, update_hbm)
    for cp in stores:
        cp.wait()


def final(merged, phat, qnext):
    shapes = ((OWN, COLS), BF16), ((COLS, ROWS), BF16), ((RANK, COLS), F32)
    return pl.pallas_call(
        final_kernel,
        out_shape=tuple(jax.ShapeDtypeStruct(*s) for s in shapes),
        in_specs=[pl.BlockSpec(memory_space=pltpu.VMEM)] * 3,
        out_specs=(pl.BlockSpec(memory_space=pl.ANY),) * 3,
        scratch_shapes=[
            *(pltpu.VMEM(*s) for s in shapes),
            pltpu.VMEM((256, RANK), F32),
            pltpu.SemaphoreType.DMA((ROWS // FINAL_LANES + 2,)),
        ],
        compiler_params=pltpu.CompilerParams(vmem_limit_bytes=24 << 20),
        name="final",
    )(*(pltpu.with_memory_space_constraint(a, pltpu.VMEM) for a in (merged, phat, qnext)))


def local(inputs, out_grads, counts, residual, q_start):
    merged, phat, qnext = chain(inputs[0], out_grads[0].T, counts, residual[0].T, q_start.T)
    update, residual_next, q_next = final(merged, phat, qnext)
    return update, residual_next.T[None], q_next.T


def solution(mesh):
    return jax.shard_map(
        local,
        mesh=mesh,
        in_specs=(
            P("dp", "mp", None),
            P("dp", None, "mp"),
            P("dp", None),
            P("dp", None, "mp"),
            P("mp", None),
        ),
        out_specs=(P("dp", "mp"), P("dp", None, "mp"), P("mp", None)),
        check_vma=False,
    )
```

```python
import functools

import jax
import jax.numpy as jnp
from jax import lax
from jax.experimental import pallas as pl
from jax.experimental.pallas import tpu as pltpu
from jax.sharding import PartitionSpec as P

MESH = pl.DeviceIdType.MESH
F32, BF16 = jnp.float32, jnp.bfloat16
NX, NY, NZ, NC = 4, 8, 8, 2
ROWS, COLS, RANK, TOK = 2560, 320, 32, 1024
HALF = RANK // NC
BLOCK = TOK // (NY * NC)
PAIR = BLOCK * NC
XL = ROWS // NX
ZR = HALF // NZ
QR = RANK // NX
QL = 384
SUB = BLOCK // 2
GRAD_LANES = 640


def far_first(*sizes):
    offsets = [()]
    for n in sizes:
        offsets = [o + (d,) for o in offsets for d in range(n)]
    return sorted(offsets, key=lambda o: -sum(min(d, n - d) for d, n in zip(o, sizes)))[:-1]


FAR_X, FAR_Y, FAR_Z = ([d for (d,) in far_first(n)] for n in (NX, NY, NZ))
FAR_PLANE = far_first(NX, NZ)
FAR_U = (4, 3, 5)
SCALE = 1.0 / 32.0
DIVISOR = 8.0
NT = (((1,), (1,)), ((), ()))
NN = (((1,), (0,)), ((), ()))
TN = (((0,), (0,)), ((), ()))


def dot(a, b, dims):
    return lax.dot_general(a, b, dims, preferred_element_type=F32)


def dot_exact(a, b, dims):
    return lax.dot_general(a, b, dims, precision=lax.Precision.HIGHEST, preferred_element_type=F32)


def split3(v):
    high = v.astype(BF16)
    rest = v - high.astype(F32)
    mid = rest.astype(BF16)
    low = (rest - mid.astype(F32)).astype(BF16)
    return jnp.concatenate([high, mid, low], axis=0)


def sum3(v):
    n = v.shape[0] // 3
    return v[:n] + (v[n : 2 * n] + v[2 * n :])


def inverse_factor(gram):
    rows = lax.broadcasted_iota(jnp.int32, (RANK, 128), 0)
    lanes = lax.broadcasted_iota(jnp.int32, (RANK, 128), 1)
    eye = jnp.where(lanes == rows + RANK, 1.0, 0.0)
    work = jnp.concatenate([gram, jnp.zeros((RANK, 128 - RANK), F32)], axis=1) + eye

    pivots = jnp.ones((RANK, 128), F32)
    for j in range(RANK):
        col = jnp.broadcast_to(work[:, j : j + 1], (RANK, 128))
        pivot = col[j : j + 1]
        pivots = jnp.where(rows == j, pivot, pivots)
        work = jnp.where(rows > j, work - col * (work[j : j + 1] / pivot), work)
    return (work / jnp.sqrt(pivots))[:, RANK : 2 * RANK]


def chain_kernel(
    inp_hbm, og_hbm, cnt_hbm, res_hbm, q_hbm,
    merged, phat_ref, qnext_ref,
    gbuf, og, cnt, res, q, wbuf,
    wq, wqin, wqh, wqr, rq, rqin, ph, ps, pr, yr, pg, pt,
    qb, qxr, qzr, qt, inv, ubuf,
    lsem, gsend, grecv, csend, crecv, cown, esend, erecv,
    wsend, wrecv, psend, precv, ysend, yrecv, pgsend, pgrecv, plane, qxsend, qxrecv, qzsend, qzrecv, qgsend, qgrecv, usend, urecv,
):
    dp, mp = lax.axis_index("dp"), lax.axis_index("mp")
    x, z = dp // NZ, lax.rem(dp, NZ)
    y, c = mp // NC, lax.rem(mp, NC)

    def at_x(i):
        return (i * NZ + z, mp)

    def at_z(i):
        return (x * NZ + i, mp)

    def at_y(i):
        return (dp, i * NC + c)

    sibling = (dp, y * NC + (1 - c))

    def other(i, d, n):
        return lax.rem(i + d, n)

    def at_dp(i):
        return (i, mp)

    def offset(dx, dz):
        return other(x, dx, NX) * NZ + other(z, dz, NZ)

    def copy(src, dst, s, r, to):
        return pltpu.make_async_remote_copy(src, dst, s, r, device_id=to, device_id_type=MESH)

    loads = [
        pltpu.make_async_copy(og_hbm, og, lsem.at[0]),
        pltpu.make_async_copy(cnt_hbm, cnt, lsem.at[1]),
        pltpu.make_async_copy(q_hbm, q, lsem.at[2]),
        pltpu.make_async_copy(inp_hbm, gbuf.at[mp], lsem.at[3]),
        pltpu.make_async_copy(res_hbm, res, lsem.at[4]),
    ]
    for load in loads:
        load.start()

    barrier = pltpu.get_barrier_semaphore()
    peers = [sibling]
    peers += [at_x(other(x, d, NX)) for d in range(1, NX)]
    peers += [at_z(other(z, d, NZ)) for d in range(1, NZ)]
    peers += [at_y(other(y, d, NY)) for d in range(1, NY)]
    for peer in peers:
        pl.semaphore_signal(barrier, inc=1, device_id=peer, device_id_type=MESH)

    loads[0].wait()
    loads[1].wait()
    loads[2].wait()
    weight = cnt[...].astype(F32) * (SCALE / DIVISOR)
    wbuf[...] = (og[...].astype(F32) * weight).astype(BF16)
    q3 = split3(q[...])
    wq[...] = sum3(dot(q3, wbuf[...], NN)).reshape(NC, HALF, TOK)
    pl.semaphore_wait(barrier, len(peers))
    for d in FAR_Z:
        pl.semaphore_signal(plane, inc=1, device_id=at_z(other(z, d, NZ)), device_id_type=MESH)

    pending = []

    def go(cp):
        cp.start()
        pending.append(cp)
        return cp

    def ring_block(up, h):
        return lax.rem(y + (NY - h if up else h), NY) * NC + c

    def ring_send(up, h, s):
        part = gbuf.at[ring_block(up, h), pl.ds(s * SUB, SUB)]
        to = at_y(other(y, 1 if up else NY - 1, NY))
        u = 0 if up else 1
        go(copy(part, part, gsend.at[u, h, s], grecv.at[u, h, s], to))

    def ring_recv(up, h, s):
        part = gbuf.at[ring_block(up, h), pl.ds(s * SUB, SUB)]
        u = 0 if up else 1
        copy(part, part, gsend.at[u, h - 1, s], grecv.at[u, h - 1, s], sibling).wait_recv()
        go(copy(part, part, csend.at[u, h - 1, s], crecv.at[u, h - 1, s], sibling))

    def ring_in(h, s):
        for up in (True, False):
            if h < NY // 2 or (s == 0) == up:
                ring_recv(up, h, s)

    def ring_out(h, s):
        for up in (True, False):
            if h < NY // 2 - 1 or (s == 0) == up:
                ring_send(up, h, s)

    def ring_sibling(h):
        for s in range(2):
            for up in (True, False):
                if h == NY // 2 and (s == 0) != up:
                    continue
                u = 0 if up else 1
                slot = lax.rem(y + (NY - h if up else h), NY) * NC + (1 - c)
                part = gbuf.at[slot, pl.ds(s * SUB, SUB)]
                copy(part, part, csend.at[u, h - 1, s], crecv.at[u, h - 1, s], sibling).wait_recv()

    def grad(ups, downs):
        chips = [lax.rem(y + NY - h, NY) for h in ups] + [lax.rem(y + h, NY) for h in downs]

        def lanes(i):
            return pl.ds(pl.multiple_of(i * PAIR, PAIR), PAIR)

        w = jnp.concatenate([wbuf[:, lanes(k)] for k in chips], axis=1)

        def step(i, carry):
            at = pl.ds(pl.multiple_of(i * GRAD_LANES, GRAD_LANES), GRAD_LANES)
            t = [gbuf[pl.ds(k * NC, NC), :, at].reshape(PAIR, GRAD_LANES) for k in chips]
            base = res[:, at].astype(F32) if ups == (0,) else merged[:, at]
            merged[:, at] = base + dot(w, jnp.concatenate(t, axis=0), NN)
            return carry

        lax.fori_loop(0, ROWS // GRAD_LANES, step, 0)

    loads[3].wait()
    own_ex = go(copy(gbuf.at[mp], gbuf.at[mp], esend.at[1], cown, sibling))
    w_ex = go(copy(wq.at[1 - c], wqin, esend.at[0], erecv.at[0], sibling))
    w_ex.wait_recv()
    wqh[...] = wq[c] + wqin[...]
    for d in FAR_Y:
        i = other(y, d, NY)
        go(copy(wqh.at[:, pl.ds(pl.multiple_of(i * PAIR, PAIR), PAIR)], wqr.at[y], wsend.at[d], wrecv.at[y], at_y(i)))

    ring_out(0, 0)
    loads[4].wait()
    rq[...] = sum3(dot(q3, res[...], NN)).reshape(NC, HALF, ROWS)
    r_ex = go(copy(rq.at[1 - c], rqin, esend.at[2], erecv.at[1], sibling))
    wqr[y] = wqh[:, pl.ds(pl.multiple_of(y * PAIR, PAIR), PAIR)]
    for d in range(1, NY):
        i = other(y, d, NY)
        copy(wqr.at[i], wqr.at[i], wsend.at[d], wrecv.at[i], sibling).wait_recv()
    ring_out(0, 1)
    w_tok = wqr[0]
    for i in range(1, NY):
        w_tok = w_tok + wqr[i]
    sib_slot = gbuf.at[y * NC + (1 - c)]
    copy(sib_slot, sib_slot, esend.at[1], cown, sibling).wait_recv()
    pair = gbuf[pl.ds(y * NC, NC)].reshape(PAIR, ROWS)
    p_tok = sum3(dot(split3(w_tok), pair, NN))
    r_ex.wait_recv()
    ph[...] = p_tok + (rq[c] + rqin[...])

    for i in range(NX):
        for k in range(NZ):
            ps[i * NZ + k] = ph[ZR * k : ZR * (k + 1), XL * i : XL * (i + 1)]
    pl.semaphore_wait(plane, NZ - 1)
    for n, (dx, dz) in enumerate(FAR_PLANE):
        i = offset(dx, dz)
        go(copy(ps.at[i], pr.at[dp], psend.at[n], precv.at[dp], at_dp(i)))
    grad((0,), ())
    ring_in(1, 0)
    pr[dp] = ps[dp]
    for dx, dz in FAR_PLANE[::-1]:
        i = offset(dx, dz)
        copy(pr.at[i], pr.at[i], psend.at[0], precv.at[i], sibling).wait_recv()
    yr[y] = jnp.sum(pr[...], axis=0)
    for d in FAR_Y:
        i = other(y, d, NY)
        go(copy(yr.at[y], yr.at[y], ysend.at[d], yrecv.at[y], at_y(i)))
    ring_in(1, 1)
    ring_sibling(1)
    grad((1,), (1,))
    for d in range(1, NY):
        i = other(y, d, NY)
        copy(yr.at[i], yr.at[i], ysend.at[d], yrecv.at[i], sibling).wait_recv()
    pg[dp] = jnp.sum(yr[...], axis=0)
    for n, (dx, dz) in enumerate(FAR_PLANE):
        i = offset(dx, dz)
        go(copy(pg.at[dp], pg.at[dp], pgsend.at[n], pgrecv.at[dp], at_dp(i)))
    ring_out(1, 0)
    ring_out(1, 1)
    ring_in(2, 0)
    ring_out(2, 0)
    for dx, dz in FAR_PLANE[::-1]:
        i = offset(dx, dz)
        copy(pg.at[i], pg.at[i], pgsend.at[0], pgrecv.at[i], sibling).wait_recv()
    for i in range(NX):
        for k in range(NZ):
            pt[c, ZR * k : ZR * (k + 1), XL * i : XL * (i + 1)] = pg[i * NZ + k]
    go(copy(pt.at[c], pt.at[c], esend.at[3], erecv.at[2], sibling))
    copy(pt.at[1 - c], pt.at[1 - c], esend.at[3], erecv.at[2], sibling).wait_recv()

    p = pt[...].reshape(RANK, ROWS)
    p3 = split3(p)

    def chip_lanes(i):
        return pl.ds(pl.multiple_of(i * PAIR, PAIR), PAIR)

    def tokens_p(i):
        ubuf[:, chip_lanes(i)] = sum3(dot(p3, gbuf[pl.ds(i * NC, NC)].reshape(PAIR, ROWS), NT))

    tokens_p(y)
    own_u = ubuf.at[:, chip_lanes(y)]
    for d in FAR_U:
        go(copy(own_u, own_u, usend.at[d], urecv.at[d], at_y(other(y, d, NY))))
    qb[...] = jnp.zeros_like(qb)
    qb[:, :COLS] = sum3(dot(p3, res[...], NT))
    tokens_p(other(y, 1, NY))
    tokens_p(other(y, NY - 1, NY))
    ring_in(2, 1)
    ring_out(2, 1)
    ring_sibling(2)
    tokens_p(other(y, 2, NY))
    tokens_p(other(y, NY - 2, NY))
    for d in FAR_U:
        theirs = ubuf.at[:, chip_lanes(other(y, NY - d, NY))]
        copy(theirs, theirs, usend.at[d], urecv.at[d], sibling).wait_recv()
    qb[:, :COLS] += sum3(dot(split3(ubuf[...]), wbuf[...], NT))
    for d in FAR_X:
        i = other(x, d, NX)
        go(copy(qb.at[pl.ds(pl.multiple_of(i * QR, QR), QR)], qxr.at[x], qxsend.at[d], qxrecv.at[x], at_x(i)))

    ring_in(3, 0)
    ring_out(3, 0)
    inv[...] = inverse_factor(dot_exact(p, p, NT))
    qxr[x] = qb[pl.ds(pl.multiple_of(x * QR, QR), QR), :]
    for d in range(1, NX):
        i = other(x, d, NX)
        copy(qxr.at[i], qxr.at[i], qxsend.at[d], qxrecv.at[i], sibling).wait_recv()
    ring_in(3, 1)
    ring_out(3, 1)
    total = qxr[0]
    for i in range(1, NX):
        total = total + qxr[i]
    qzr[z] = total
    for d in FAR_Z:
        i = other(z, d, NZ)
        go(copy(qzr.at[z], qzr.at[z], qzsend.at[d], qzrecv.at[z], at_z(i)))
    grad((2,), (2,))
    ring_sibling(3)
    grad((3,), (3,))
    for d in range(1, NZ):
        i = other(z, d, NZ)
        copy(qzr.at[i], qzr.at[i], qzsend.at[d], qzrecv.at[i], sibling).wait_recv()
    total = qzr[0]
    for i in range(1, NZ):
        total = total + qzr[i]
    qt[x] = total
    for d in FAR_X:
        i = other(x, d, NX)
        go(copy(qt.at[x], qt.at[x], qgsend.at[d], qgrecv.at[x], at_x(i)))
    phat_ref[...] = dot_exact(inv[...], p, NN)
    ring_in(4, 0)
    ring_in(4, 1)
    ring_sibling(4)
    grad((), (4,))
    for d in range(1, NX):
        i = other(x, d, NX)
        copy(qt.at[i], qt.at[i], qgsend.at[d], qgrecv.at[i], sibling).wait_recv()
    qnext_ref[...] = dot_exact(inv[...], qt[...].reshape(RANK, QL), NN)
    for cp in pending:
        cp.wait_send()


def chain(inputs, out_grads, counts, residual, q_start):
    dma = pltpu.SemaphoreType.DMA
    vmem = pltpu.VMEM
    return pl.pallas_call(
        chain_kernel,
        out_shape=(
            vmem((COLS, ROWS), F32),
            vmem((RANK, ROWS), F32),
            vmem((RANK, QL), F32),
        ),
        in_specs=[pl.BlockSpec(memory_space=pl.ANY)] * 5,
        out_specs=(
            pl.BlockSpec(memory_space=pltpu.VMEM),
            pl.BlockSpec(memory_space=pltpu.VMEM),
            pl.BlockSpec(memory_space=pltpu.VMEM),
        ),
        scratch_shapes=[
            vmem((NY * NC, BLOCK, ROWS), BF16),
            vmem((COLS, TOK), BF16),
            vmem((1, TOK), jnp.int32),
            vmem((COLS, ROWS), BF16),
            vmem((RANK, COLS), F32),
            vmem((COLS, TOK), BF16),
            vmem((NC, HALF, TOK), F32),
            vmem((HALF, TOK), F32),
            vmem((HALF, TOK), F32),
            vmem((NY, HALF, PAIR), F32),
            vmem((NC, HALF, ROWS), F32),
            vmem((HALF, ROWS), F32),
            vmem((HALF, ROWS), F32),
            vmem((NX * NZ, ZR, XL), F32),
            vmem((NX * NZ, ZR, XL), F32),
            vmem((NY, ZR, XL), F32),
            vmem((NX * NZ, ZR, XL), F32),
            vmem((NC, HALF, ROWS), F32),
            vmem((RANK, QL), F32),
            vmem((NX, QR, QL), F32),
            vmem((NZ, QR, QL), F32),
            vmem((NX, QR, QL), F32),
            vmem((RANK, RANK), F32),
            vmem((RANK, TOK), F32),
            dma((5,)),
            dma((2, 4, 2)), dma((2, 4, 2)),
            dma((2, 4, 2)), dma((2, 4, 2)),
            dma,
            dma((4,)), dma((3,)),
            dma((NY,)), dma((NY,)),
            dma((NX * NZ,)), dma((NX * NZ,)),
            dma((NY,)), dma((NY,)),
            dma((NX * NZ,)), dma((NX * NZ,)),
            pltpu.SemaphoreType.REGULAR,
            dma((NX,)), dma((NX,)),
            dma((NZ,)), dma((NZ,)),
            dma((NX,)), dma((NX,)),
            dma((NY,)), dma((NY,)),
        ],
        compiler_params=pltpu.CompilerParams(
            collective_id=0, has_side_effects=True, vmem_limit_bytes=40 << 20
        ),
        name="chain",
    )(*(pltpu.with_memory_space_constraint(a, pltpu.HBM) for a in (inputs, out_grads, counts, residual, q_start)))


FINAL_LANES = 640
OWN = ROWS // (NX * NZ)


def final_kernel(
    merged_ref, phat_ref, qnext_ref, update_hbm, res_hbm, q_hbm,
    update, res, q, turned, sems,
):
    def high_low(v):
        high = v.astype(BF16)
        return high, (v - high.astype(F32)).astype(BF16)

    stores = []

    def store(src, dst):
        stores.append(pltpu.make_async_copy(src, dst, sems.at[len(stores)]))
        stores[-1].start()

    q[...] = qnext_ref[:, :COLS]
    store(q, q_hbm)
    high, low = high_low(qnext_ref[...].T)
    q_cols = jnp.concatenate([high, low, high], axis=1)[:COLS]
    for i in range(ROWS // FINAL_LANES):
        at = slice(i * FINAL_LANES, (i + 1) * FINAL_LANES)
        high, low = high_low(phat_ref[:, at])
        block = dot(q_cols, jnp.concatenate([high, high, low], axis=0), NN)
        res[:, at] = (merged_ref[:, at] - block * (1.0 / (NX * NZ))).astype(BF16)
        store(res.at[:, at], res_hbm.at[:, at])
    first = lax.axis_index("dp") * OWN
    base = jnp.minimum(first // 128, ROWS // 128 - 2) * 128
    turned[...] = phat_ref[:, pl.ds(pl.multiple_of(base, 128), 256)].T
    high, low = high_low(turned[pl.ds(pl.multiple_of(first - base, 8), OWN), :])
    update[...] = dot(jnp.concatenate([high, high, low], axis=1), q_cols, NT).astype(BF16)
    store(update, update_hbm)
    for cp in stores:
        cp.wait()


def final(merged, phat, qnext):
    shapes = ((OWN, COLS), BF16), ((COLS, ROWS), BF16), ((RANK, COLS), F32)
    return pl.pallas_call(
        final_kernel,
        out_shape=tuple(jax.ShapeDtypeStruct(*s) for s in shapes),
        in_specs=[pl.BlockSpec(memory_space=pltpu.VMEM)] * 3,
        out_specs=(pl.BlockSpec(memory_space=pl.ANY),) * 3,
        scratch_shapes=[
            *(pltpu.VMEM(*s) for s in shapes),
            pltpu.VMEM((256, RANK), F32),
            pltpu.SemaphoreType.DMA((ROWS // FINAL_LANES + 2,)),
        ],
        compiler_params=pltpu.CompilerParams(vmem_limit_bytes=24 << 20),
        name="final",
    )(*(pltpu.with_memory_space_constraint(a, pltpu.VMEM) for a in (merged, phat, qnext)))


def local(inputs, out_grads, counts, residual, q_start):
    merged, phat, qnext = chain(inputs[0], out_grads[0].T, counts, residual[0].T, q_start.T)
    update, residual_next, q_next = final(merged, phat, qnext)
    return update, residual_next.T[None], q_next.T


def solution(mesh):
    return jax.shard_map(
        local,
        mesh=mesh,
        in_specs=(
            P("dp", "mp", None),
            P("dp", None, "mp"),
            P("dp", None),
            P("dp", None, "mp"),
            P("mp", None),
        ),
        out_specs=(P("dp", "mp"), P("dp", None, "mp"), P("mp", None)),
        check_vma=False,
    )
```

```python
import functools

import jax
import jax.numpy as jnp
from jax import lax
from jax.experimental import pallas as pl
from jax.experimental.pallas import tpu as pltpu
from jax.sharding import PartitionSpec as P

MESH = pl.DeviceIdType.MESH
F32, BF16 = jnp.float32, jnp.bfloat16
NX, NY, NZ, NC = 4, 8, 8, 2
ROWS, COLS, RANK, TOK = 2560, 320, 32, 1024
HALF = RANK // NC
BLOCK = TOK // (NY * NC)
PAIR = BLOCK * NC
XL = ROWS // NX
ZR = HALF // NZ
QR = RANK // NX
QL = 384
SUB = BLOCK // 2
PANEL = 4
GRAD_LANES = 1280


def far_first(*sizes):
    offsets = [()]
    for n in sizes:
        offsets = [o + (d,) for o in offsets for d in range(n)]
    return sorted(offsets, key=lambda o: -sum(min(d, n - d) for d, n in zip(o, sizes)))[:-1]


FAR_X, FAR_Y, FAR_Z = ([d for (d,) in far_first(n)] for n in (NX, NY, NZ))
FAR_PLANE = far_first(NX, NZ)
FAR_U = (4, 3, 5)
SCALE = 1.0 / 32.0
DIVISOR = 8.0
NT = (((1,), (1,)), ((), ()))
NN = (((1,), (0,)), ((), ()))
TN = (((0,), (0,)), ((), ()))


def dot(a, b, dims):
    return lax.dot_general(a, b, dims, preferred_element_type=F32)


def dot_exact(a, b, dims):
    return lax.dot_general(a, b, dims, precision=lax.Precision.HIGHEST, preferred_element_type=F32)


def split3(v):
    high = v.astype(BF16)
    rest = v - high.astype(F32)
    mid = rest.astype(BF16)
    low = (rest - mid.astype(F32)).astype(BF16)
    return jnp.concatenate([high, mid, low], axis=0)


def sum3(v):
    n = v.shape[0] // 3
    return v[:n] + (v[n : 2 * n] + v[2 * n :])


def inverse_factor(gram):
    rows = lax.broadcasted_iota(jnp.int32, (RANK, 128), 0)
    lanes = lax.broadcasted_iota(jnp.int32, (RANK, 128), 1)
    eye = jnp.where(lanes == rows + RANK, 1.0, 0.0)
    work = jnp.concatenate([gram, jnp.zeros((RANK, 128 - RANK), F32)], axis=1) + eye

    pivots = jnp.ones((RANK, 128), F32)
    for first in range(0, RANK, PANEL):
        cols = [jnp.broadcast_to(work[:, j : j + 1], (RANK, 128)) for j in range(first, first + PANEL)]
        for k in range(PANEL):
            j = first + k
            pivot = cols[k][j : j + 1]
            pivots = jnp.where(rows == j, pivot, pivots)
            below = jnp.where(rows > j, cols[k], 0.0) * (1.0 / pivot)
            work = work - below * work[j : j + 1]
            cols = [cols[m] - below * cols[m][j : j + 1] if m > k else cols[m] for m in range(PANEL)]
    return (work / jnp.sqrt(pivots))[:, RANK : 2 * RANK]


def chain_kernel(
    inp_hbm, og_hbm, cnt_hbm, res_hbm, q_hbm,
    merged, phat_ref, qnext_ref,
    gbuf, og, cnt, res, q, wbuf,
    wq, wqin, wqh, wqr, rq, rqin, ph, ps, pr, yr, pg, pt,
    qb, qxr, qzr, qt, inv, ubuf,
    lsem, gsend, grecv, csend, crecv, cown, esend, erecv,
    wsend, wrecv, psend, precv, ysend, yrecv, pgsend, pgrecv, plane, qxsend, qxrecv, qzsend, qzrecv, qgsend, qgrecv, usend, urecv,
):
    dp, mp = lax.axis_index("dp"), lax.axis_index("mp")
    x, z = dp // NZ, lax.rem(dp, NZ)
    y, c = mp // NC, lax.rem(mp, NC)

    def at_x(i):
        return (i * NZ + z, mp)

    def at_z(i):
        return (x * NZ + i, mp)

    def at_y(i):
        return (dp, i * NC + c)

    sibling = (dp, y * NC + (1 - c))

    def other(i, d, n):
        return lax.rem(i + d, n)

    def at_dp(i):
        return (i, mp)

    def offset(dx, dz):
        return other(x, dx, NX) * NZ + other(z, dz, NZ)

    def copy(src, dst, s, r, to):
        return pltpu.make_async_remote_copy(src, dst, s, r, device_id=to, device_id_type=MESH)

    loads = [
        pltpu.make_async_copy(og_hbm, og, lsem.at[0]),
        pltpu.make_async_copy(cnt_hbm, cnt, lsem.at[1]),
        pltpu.make_async_copy(q_hbm, q, lsem.at[2]),
        pltpu.make_async_copy(inp_hbm, gbuf.at[mp], lsem.at[3]),
        pltpu.make_async_copy(res_hbm, res, lsem.at[4]),
    ]
    for load in loads:
        load.start()

    barrier = pltpu.get_barrier_semaphore()
    peers = [sibling]
    peers += [at_x(other(x, d, NX)) for d in range(1, NX)]
    peers += [at_z(other(z, d, NZ)) for d in range(1, NZ)]
    peers += [at_y(other(y, d, NY)) for d in range(1, NY)]
    for peer in peers:
        pl.semaphore_signal(barrier, inc=1, device_id=peer, device_id_type=MESH)

    loads[0].wait()
    loads[1].wait()
    loads[2].wait()
    weight = cnt[...].astype(F32) * (SCALE / DIVISOR)
    wbuf[...] = (og[...].astype(F32) * weight).astype(BF16)
    q3 = split3(q[...])
    wq[...] = sum3(dot(q3, wbuf[...], NN)).reshape(NC, HALF, TOK)
    pl.semaphore_wait(barrier, len(peers))
    for d in FAR_Z:
        pl.semaphore_signal(plane, inc=1, device_id=at_z(other(z, d, NZ)), device_id_type=MESH)

    pending = []

    def go(cp):
        cp.start()
        pending.append(cp)
        return cp

    def ring_block(up, h):
        return lax.rem(y + (NY - h if up else h), NY) * NC + c

    def ring_send(up, h, s):
        part = gbuf.at[ring_block(up, h), pl.ds(s * SUB, SUB)]
        to = at_y(other(y, 1 if up else NY - 1, NY))
        u = 0 if up else 1
        go(copy(part, part, gsend.at[u, h, s], grecv.at[u, h, s], to))

    def ring_recv(up, h, s):
        part = gbuf.at[ring_block(up, h), pl.ds(s * SUB, SUB)]
        u = 0 if up else 1
        copy(part, part, gsend.at[u, h - 1, s], grecv.at[u, h - 1, s], sibling).wait_recv()
        go(copy(part, part, csend.at[u, h - 1, s], crecv.at[u, h - 1, s], sibling))

    def ring_in(h, s):
        for up in (True, False):
            if h < NY // 2 or (s == 0) == up:
                ring_recv(up, h, s)

    def ring_out(h, s):
        for up in (True, False):
            if h < NY // 2 - 1 or (s == 0) == up:
                ring_send(up, h, s)

    def ring_sibling(h):
        for s in range(2):
            for up in (True, False):
                if h == NY // 2 and (s == 0) != up:
                    continue
                u = 0 if up else 1
                slot = lax.rem(y + (NY - h if up else h), NY) * NC + (1 - c)
                part = gbuf.at[slot, pl.ds(s * SUB, SUB)]
                copy(part, part, csend.at[u, h - 1, s], crecv.at[u, h - 1, s], sibling).wait_recv()

    def grad(ups, downs):
        chips = [lax.rem(y + NY - h, NY) for h in ups] + [lax.rem(y + h, NY) for h in downs]

        def lanes(i):
            return pl.ds(pl.multiple_of(i * PAIR, PAIR), PAIR)

        w = jnp.concatenate([wbuf[:, lanes(k)] for k in chips], axis=1)

        def step(i, carry):
            at = pl.ds(pl.multiple_of(i * GRAD_LANES, GRAD_LANES), GRAD_LANES)
            t = [gbuf[pl.ds(k * NC, NC), :, at].reshape(PAIR, GRAD_LANES) for k in chips]
            base = res[:, at].astype(F32) if ups == (0,) else merged[:, at]
            merged[:, at] = base + dot(w, jnp.concatenate(t, axis=0), NN)
            return carry

        lax.fori_loop(0, ROWS // GRAD_LANES, step, 0)

    loads[3].wait()
    own_ex = go(copy(gbuf.at[mp], gbuf.at[mp], esend.at[1], cown, sibling))
    w_ex = go(copy(wq.at[1 - c], wqin, esend.at[0], erecv.at[0], sibling))
    w_ex.wait_recv()
    wqh[...] = wq[c] + wqin[...]
    for d in FAR_Y:
        i = other(y, d, NY)
        go(copy(wqh.at[:, pl.ds(pl.multiple_of(i * PAIR, PAIR), PAIR)], wqr.at[y], wsend.at[d], wrecv.at[y], at_y(i)))

    ring_out(0, 0)
    loads[4].wait()
    rq[...] = sum3(dot(q3, res[...], NN)).reshape(NC, HALF, ROWS)
    r_ex = go(copy(rq.at[1 - c], rqin, esend.at[2], erecv.at[1], sibling))
    wqr[y] = wqh[:, pl.ds(pl.multiple_of(y * PAIR, PAIR), PAIR)]
    for d in range(1, NY):
        i = other(y, d, NY)
        copy(wqr.at[i], wqr.at[i], wsend.at[d], wrecv.at[i], sibling).wait_recv()
    ring_out(0, 1)
    w_tok = wqr[0]
    for i in range(1, NY):
        w_tok = w_tok + wqr[i]
    sib_slot = gbuf.at[y * NC + (1 - c)]
    copy(sib_slot, sib_slot, esend.at[1], cown, sibling).wait_recv()
    pair = gbuf[pl.ds(y * NC, NC)].reshape(PAIR, ROWS)
    p_tok = sum3(dot(split3(w_tok), pair, NN))
    r_ex.wait_recv()
    ph[...] = p_tok + (rq[c] + rqin[...])

    for i in range(NX):
        for k in range(NZ):
            ps[i * NZ + k] = ph[ZR * k : ZR * (k + 1), XL * i : XL * (i + 1)]
    pl.semaphore_wait(plane, NZ - 1)
    for n, (dx, dz) in enumerate(FAR_PLANE):
        i = offset(dx, dz)
        go(copy(ps.at[i], pr.at[dp], psend.at[n], precv.at[dp], at_dp(i)))
    ring_in(1, 0)
    ring_out(1, 0)
    grad((0,), ())
    pr[dp] = ps[dp]
    for dx, dz in FAR_PLANE[::-1]:
        i = offset(dx, dz)
        copy(pr.at[i], pr.at[i], psend.at[0], precv.at[i], sibling).wait_recv()
    yr[y] = jnp.sum(pr[...], axis=0)
    for d in FAR_Y:
        i = other(y, d, NY)
        go(copy(yr.at[y], yr.at[y], ysend.at[d], yrecv.at[y], at_y(i)))
    ring_in(1, 1)
    ring_sibling(1)
    grad((1,), (1,))
    for d in range(1, NY):
        i = other(y, d, NY)
        copy(yr.at[i], yr.at[i], ysend.at[d], yrecv.at[i], sibling).wait_recv()
    pg[dp] = jnp.sum(yr[...], axis=0)
    for n, (dx, dz) in enumerate(FAR_PLANE):
        i = offset(dx, dz)
        go(copy(pg.at[dp], pg.at[dp], pgsend.at[n], pgrecv.at[dp], at_dp(i)))
    ring_out(1, 1)
    ring_in(2, 0)
    ring_out(2, 0)
    for dx, dz in FAR_PLANE[::-1]:
        i = offset(dx, dz)
        copy(pg.at[i], pg.at[i], pgsend.at[0], pgrecv.at[i], sibling).wait_recv()
    for i in range(NX):
        for k in range(NZ):
            pt[c, ZR * k : ZR * (k + 1), XL * i : XL * (i + 1)] = pg[i * NZ + k]
    go(copy(pt.at[c], pt.at[c], esend.at[3], erecv.at[2], sibling))
    copy(pt.at[1 - c], pt.at[1 - c], esend.at[3], erecv.at[2], sibling).wait_recv()

    p = pt[...].reshape(RANK, ROWS)
    p3 = split3(p)

    def chip_lanes(i):
        return pl.ds(pl.multiple_of(i * PAIR, PAIR), PAIR)

    def tokens_p(i):
        ubuf[:, chip_lanes(i)] = sum3(dot(p3, gbuf[pl.ds(i * NC, NC)].reshape(PAIR, ROWS), NT))

    tokens_p(y)
    own_u = ubuf.at[:, chip_lanes(y)]
    for d in FAR_U:
        go(copy(own_u, own_u, usend.at[d], urecv.at[d], at_y(other(y, d, NY))))
    qb[...] = jnp.zeros_like(qb)
    qb[:, :COLS] = sum3(dot(p3, res[...], NT))
    tokens_p(other(y, 1, NY))
    tokens_p(other(y, NY - 1, NY))
    ring_in(2, 1)
    ring_out(2, 1)
    ring_sibling(2)
    tokens_p(other(y, 2, NY))
    tokens_p(other(y, NY - 2, NY))
    for d in FAR_U:
        theirs = ubuf.at[:, chip_lanes(other(y, NY - d, NY))]
        copy(theirs, theirs, usend.at[d], urecv.at[d], sibling).wait_recv()
    qb[:, :COLS] += sum3(dot(split3(ubuf[...]), wbuf[...], NT))
    for d in FAR_X:
        i = other(x, d, NX)
        go(copy(qb.at[pl.ds(pl.multiple_of(i * QR, QR), QR)], qxr.at[x], qxsend.at[d], qxrecv.at[x], at_x(i)))

    ring_in(3, 0)
    ring_out(3, 0)
    inv[...] = inverse_factor(dot_exact(p, p, NT))
    qxr[x] = qb[pl.ds(pl.multiple_of(x * QR, QR), QR), :]
    for d in range(1, NX):
        i = other(x, d, NX)
        copy(qxr.at[i], qxr.at[i], qxsend.at[d], qxrecv.at[i], sibling).wait_recv()
    ring_in(3, 1)
    ring_out(3, 1)
    total = qxr[0]
    for i in range(1, NX):
        total = total + qxr[i]
    qzr[z] = total
    for d in FAR_Z:
        i = other(z, d, NZ)
        go(copy(qzr.at[z], qzr.at[z], qzsend.at[d], qzrecv.at[z], at_z(i)))
    grad((2,), (2,))
    ring_sibling(3)
    grad((3,), (3,))
    for d in range(1, NZ):
        i = other(z, d, NZ)
        copy(qzr.at[i], qzr.at[i], qzsend.at[d], qzrecv.at[i], sibling).wait_recv()
    total = qzr[0]
    for i in range(1, NZ):
        total = total + qzr[i]
    qt[x] = total
    for d in FAR_X:
        i = other(x, d, NX)
        go(copy(qt.at[x], qt.at[x], qgsend.at[d], qgrecv.at[x], at_x(i)))
    phat_ref[...] = dot_exact(inv[...], p, NN)
    ring_in(4, 0)
    ring_in(4, 1)
    ring_sibling(4)
    grad((), (4,))
    for d in range(1, NX):
        i = other(x, d, NX)
        copy(qt.at[i], qt.at[i], qgsend.at[d], qgrecv.at[i], sibling).wait_recv()
    qnext_ref[...] = dot_exact(inv[...], qt[...].reshape(RANK, QL), NN)
    for cp in pending:
        cp.wait_send()


def chain(inputs, out_grads, counts, residual, q_start):
    dma = pltpu.SemaphoreType.DMA
    vmem = pltpu.VMEM
    return pl.pallas_call(
        chain_kernel,
        out_shape=(
            vmem((COLS, ROWS), F32),
            vmem((RANK, ROWS), F32),
            vmem((RANK, QL), F32),
        ),
        in_specs=[pl.BlockSpec(memory_space=pl.ANY)] * 5,
        out_specs=(
            pl.BlockSpec(memory_space=pltpu.VMEM),
            pl.BlockSpec(memory_space=pltpu.VMEM),
            pl.BlockSpec(memory_space=pltpu.VMEM),
        ),
        scratch_shapes=[
            vmem((NY * NC, BLOCK, ROWS), BF16),
            vmem((COLS, TOK), BF16),
            vmem((1, TOK), jnp.int32),
            vmem((COLS, ROWS), BF16),
            vmem((RANK, COLS), F32),
            vmem((COLS, TOK), BF16),
            vmem((NC, HALF, TOK), F32),
            vmem((HALF, TOK), F32),
            vmem((HALF, TOK), F32),
            vmem((NY, HALF, PAIR), F32),
            vmem((NC, HALF, ROWS), F32),
            vmem((HALF, ROWS), F32),
            vmem((HALF, ROWS), F32),
            vmem((NX * NZ, ZR, XL), F32),
            vmem((NX * NZ, ZR, XL), F32),
            vmem((NY, ZR, XL), F32),
            vmem((NX * NZ, ZR, XL), F32),
            vmem((NC, HALF, ROWS), F32),
            vmem((RANK, QL), F32),
            vmem((NX, QR, QL), F32),
            vmem((NZ, QR, QL), F32),
            vmem((NX, QR, QL), F32),
            vmem((RANK, RANK), F32),
            vmem((RANK, TOK), F32),
            dma((5,)),
            dma((2, 4, 2)), dma((2, 4, 2)),
            dma((2, 4, 2)), dma((2, 4, 2)),
            dma,
            dma((4,)), dma((3,)),
            dma((NY,)), dma((NY,)),
            dma((NX * NZ,)), dma((NX * NZ,)),
            dma((NY,)), dma((NY,)),
            dma((NX * NZ,)), dma((NX * NZ,)),
            pltpu.SemaphoreType.REGULAR,
            dma((NX,)), dma((NX,)),
            dma((NZ,)), dma((NZ,)),
            dma((NX,)), dma((NX,)),
            dma((NY,)), dma((NY,)),
        ],
        compiler_params=pltpu.CompilerParams(
            collective_id=0, has_side_effects=True, vmem_limit_bytes=40 << 20
        ),
        name="chain",
    )(*(pltpu.with_memory_space_constraint(a, pltpu.HBM) for a in (inputs, out_grads, counts, residual, q_start)))


FINAL_LANES = 640
OWN = ROWS // (NX * NZ)


def final_kernel(
    merged_ref, phat_ref, qnext_ref, update_hbm, res_hbm, q_hbm,
    update, res, q, turned, sems,
):
    def high_low(v):
        high = v.astype(BF16)
        return high, (v - high.astype(F32)).astype(BF16)

    stores = []

    def store(src, dst):
        stores.append(pltpu.make_async_copy(src, dst, sems.at[len(stores)]))
        stores[-1].start()

    q[...] = qnext_ref[:, :COLS]
    store(q, q_hbm)
    high, low = high_low(qnext_ref[...].T)
    q_cols = jnp.concatenate([high, low, high], axis=1)[:COLS]
    for i in range(ROWS // FINAL_LANES):
        at = slice(i * FINAL_LANES, (i + 1) * FINAL_LANES)
        high, low = high_low(phat_ref[:, at])
        block = dot(q_cols, jnp.concatenate([high, high, low], axis=0), NN)
        res[:, at] = (merged_ref[:, at] - block * (1.0 / (NX * NZ))).astype(BF16)
        store(res.at[:, at], res_hbm.at[:, at])
    first = lax.axis_index("dp") * OWN
    base = jnp.minimum(first // 128, ROWS // 128 - 2) * 128
    turned[...] = phat_ref[:, pl.ds(pl.multiple_of(base, 128), 256)].T
    high, low = high_low(turned[pl.ds(pl.multiple_of(first - base, 8), OWN), :])
    update[...] = dot(jnp.concatenate([high, high, low], axis=1), q_cols, NT).astype(BF16)
    store(update, update_hbm)
    for cp in stores:
        cp.wait()


def final(merged, phat, qnext):
    shapes = ((OWN, COLS), BF16), ((COLS, ROWS), BF16), ((RANK, COLS), F32)
    return pl.pallas_call(
        final_kernel,
        out_shape=tuple(jax.ShapeDtypeStruct(*s) for s in shapes),
        in_specs=[pl.BlockSpec(memory_space=pltpu.VMEM)] * 3,
        out_specs=(pl.BlockSpec(memory_space=pl.ANY),) * 3,
        scratch_shapes=[
            *(pltpu.VMEM(*s) for s in shapes),
            pltpu.VMEM((256, RANK), F32),
            pltpu.SemaphoreType.DMA((ROWS // FINAL_LANES + 2,)),
        ],
        compiler_params=pltpu.CompilerParams(vmem_limit_bytes=24 << 20),
        name="final",
    )(*(pltpu.with_memory_space_constraint(a, pltpu.VMEM) for a in (merged, phat, qnext)))


def local(inputs, out_grads, counts, residual, q_start):
    merged, phat, qnext = chain(inputs[0], out_grads[0].T, counts, residual[0].T, q_start.T)
    update, residual_next, q_next = final(merged, phat, qnext)
    return update, residual_next.T[None], q_next.T


def solution(mesh):
    return jax.shard_map(
        local,
        mesh=mesh,
        in_specs=(
            P("dp", "mp", None),
            P("dp", None, "mp"),
            P("dp", None),
            P("dp", None, "mp"),
            P("mp", None),
        ),
        out_specs=(P("dp", "mp"), P("dp", None, "mp"), P("mp", None)),
        check_vma=False,
    )
```

```python
import functools

import jax
import jax.numpy as jnp
from jax import lax
from jax.experimental import pallas as pl
from jax.experimental.pallas import tpu as pltpu
from jax.sharding import PartitionSpec as P

MESH = pl.DeviceIdType.MESH
F32, BF16 = jnp.float32, jnp.bfloat16
NX, NY, NZ, NC = 4, 8, 8, 2
ROWS, COLS, RANK, TOK = 2560, 320, 32, 1024
HALF = RANK // NC
BLOCK = TOK // (NY * NC)
PAIR = BLOCK * NC
XL = ROWS // NX
ZR = HALF // NZ
QR = RANK // NX
QL = 384
SUB = BLOCK // 2
PANEL = 4
GRAD_LANES = 1280


def far_first(*sizes):
    offsets = [()]
    for n in sizes:
        offsets = [o + (d,) for o in offsets for d in range(n)]
    return sorted(offsets, key=lambda o: -sum(min(d, n - d) for d, n in zip(o, sizes)))[:-1]


FAR_X, FAR_Y, FAR_Z = ([d for (d,) in far_first(n)] for n in (NX, NY, NZ))
FAR_PLANE = far_first(NX, NZ)
FAR_U = (4, 3, 5)
SCALE = 1.0 / 32.0
DIVISOR = 8.0
NT = (((1,), (1,)), ((), ()))
NN = (((1,), (0,)), ((), ()))
TN = (((0,), (0,)), ((), ()))


def dot(a, b, dims):
    return lax.dot_general(a, b, dims, preferred_element_type=F32)


def dot_exact(a, b, dims):
    return lax.dot_general(a, b, dims, precision=lax.Precision.HIGHEST, preferred_element_type=F32)


def split3(v):
    high = v.astype(BF16)
    rest = v - high.astype(F32)
    mid = rest.astype(BF16)
    low = (rest - mid.astype(F32)).astype(BF16)
    return jnp.concatenate([high, mid, low], axis=0)


def sum3(v):
    n = v.shape[0] // 3
    return v[:n] + (v[n : 2 * n] + v[2 * n :])


def inverse_factor(gram):
    rows = lax.broadcasted_iota(jnp.int32, (RANK, 128), 0)
    lanes = lax.broadcasted_iota(jnp.int32, (RANK, 128), 1)
    eye = jnp.where(lanes == rows + RANK, 1.0, 0.0)
    work = jnp.concatenate([gram, jnp.zeros((RANK, 128 - RANK), F32)], axis=1) + eye

    pivots = jnp.ones((RANK, 128), F32)
    for first in range(0, RANK, PANEL):
        cols = [jnp.broadcast_to(work[:, j : j + 1], (RANK, 128)) for j in range(first, first + PANEL)]
        for k in range(PANEL):
            j = first + k
            pivot = cols[k][j : j + 1]
            pivots = jnp.where(rows == j, pivot, pivots)
            below = jnp.where(rows > j, cols[k], 0.0) * (1.0 / pivot)
            work = work - below * work[j : j + 1]
            cols = [cols[m] - below * cols[m][j : j + 1] if m > k else cols[m] for m in range(PANEL)]
    return (work / jnp.sqrt(pivots))[:, RANK : 2 * RANK]


def chain_kernel(
    inp_hbm, og_hbm, cnt_hbm, res_hbm, q_hbm,
    merged, phat_ref, qnext_ref,
    gbuf, og, cnt, res, q, wbuf,
    wq, wqin, wqh, wqr, rq, rqin, ph, ps, pr, yr, pg, pt,
    qb, qxr, qzr, qt, inv, ubuf,
    lsem, gsend, grecv, csend, crecv, cown, esend, erecv,
    wsend, wrecv, psend, precv, ysend, yrecv, pgsend, pgrecv, plane, qxsend, qxrecv, qzsend, qzrecv, qgsend, qgrecv, usend, urecv,
):
    dp, mp = lax.axis_index("dp"), lax.axis_index("mp")
    x, z = dp // NZ, lax.rem(dp, NZ)
    y, c = mp // NC, lax.rem(mp, NC)

    def at_x(i):
        return (i * NZ + z, mp)

    def at_z(i):
        return (x * NZ + i, mp)

    def at_y(i):
        return (dp, i * NC + c)

    sibling = (dp, y * NC + (1 - c))

    def other(i, d, n):
        return lax.rem(i + d, n)

    def at_dp(i):
        return (i, mp)

    def offset(dx, dz):
        return other(x, dx, NX) * NZ + other(z, dz, NZ)

    def copy(src, dst, s, r, to):
        return pltpu.make_async_remote_copy(src, dst, s, r, device_id=to, device_id_type=MESH)

    loads = [
        pltpu.make_async_copy(og_hbm, og, lsem.at[0]),
        pltpu.make_async_copy(cnt_hbm, cnt, lsem.at[1]),
        pltpu.make_async_copy(q_hbm, q, lsem.at[2]),
        pltpu.make_async_copy(inp_hbm, gbuf.at[mp], lsem.at[3]),
        pltpu.make_async_copy(res_hbm, res, lsem.at[4]),
    ]
    for load in loads[:3]:
        load.start()

    barrier = pltpu.get_barrier_semaphore()
    peers = [at_y(other(y, d, NY)) for d in FAR_Y] + [sibling]
    peers += [at_x(other(x, d, NX)) for d in range(1, NX)]
    peers += [at_z(other(z, d, NZ)) for d in range(1, NZ)]
    for peer in peers:
        pl.semaphore_signal(barrier, inc=1, device_id=peer, device_id_type=MESH)
    for load in loads[3:]:
        load.start()

    loads[0].wait()
    loads[1].wait()
    loads[2].wait()
    weight = cnt[...].astype(F32) * (SCALE / DIVISOR)
    wbuf[...] = (og[...].astype(F32) * weight).astype(BF16)
    q3 = split3(q[...])
    wq[...] = sum3(dot(q3, wbuf[...], NN)).reshape(NC, HALF, TOK)
    pl.semaphore_wait(barrier, len(peers))
    for d in FAR_Z:
        pl.semaphore_signal(plane, inc=1, device_id=at_z(other(z, d, NZ)), device_id_type=MESH)

    pending = []

    def go(cp):
        cp.start()
        pending.append(cp)
        return cp

    def ring_block(up, h):
        return lax.rem(y + (NY - h if up else h), NY) * NC + c

    def ring_send(up, h, s):
        part = gbuf.at[ring_block(up, h), pl.ds(s * SUB, SUB)]
        to = at_y(other(y, 1 if up else NY - 1, NY))
        u = 0 if up else 1
        go(copy(part, part, gsend.at[u, h, s], grecv.at[u, h, s], to))

    def ring_recv(up, h, s):
        part = gbuf.at[ring_block(up, h), pl.ds(s * SUB, SUB)]
        u = 0 if up else 1
        copy(part, part, gsend.at[u, h - 1, s], grecv.at[u, h - 1, s], sibling).wait_recv()
        go(copy(part, part, csend.at[u, h - 1, s], crecv.at[u, h - 1, s], sibling))

    def ring_in(h, s):
        for up in (True, False):
            if h < NY // 2 or (s == 0) == up:
                ring_recv(up, h, s)

    def ring_out(h, s):
        for up in (True, False):
            if h < NY // 2 - 1 or (s == 0) == up:
                ring_send(up, h, s)

    def ring_sibling(h):
        for s in range(2):
            for up in (True, False):
                if h == NY // 2 and (s == 0) != up:
                    continue
                u = 0 if up else 1
                slot = lax.rem(y + (NY - h if up else h), NY) * NC + (1 - c)
                part = gbuf.at[slot, pl.ds(s * SUB, SUB)]
                copy(part, part, csend.at[u, h - 1, s], crecv.at[u, h - 1, s], sibling).wait_recv()

    def grad(ups, downs):
        chips = [lax.rem(y + NY - h, NY) for h in ups] + [lax.rem(y + h, NY) for h in downs]

        def lanes(i):
            return pl.ds(pl.multiple_of(i * PAIR, PAIR), PAIR)

        w = jnp.concatenate([wbuf[:, lanes(k)] for k in chips], axis=1)

        def step(i, carry):
            at = pl.ds(pl.multiple_of(i * GRAD_LANES, GRAD_LANES), GRAD_LANES)
            t = [gbuf[pl.ds(k * NC, NC), :, at].reshape(PAIR, GRAD_LANES) for k in chips]
            base = res[:, at].astype(F32) if ups == (0,) else merged[:, at]
            merged[:, at] = base + dot(w, jnp.concatenate(t, axis=0), NN)
            return carry

        lax.fori_loop(0, ROWS // GRAD_LANES, step, 0)

    loads[3].wait()
    own_ex = go(copy(gbuf.at[mp], gbuf.at[mp], esend.at[1], cown, sibling))
    w_ex = go(copy(wq.at[1 - c], wqin, esend.at[0], erecv.at[0], sibling))
    w_ex.wait_recv()
    wqh[...] = wq[c] + wqin[...]
    for d in FAR_Y:
        i = other(y, d, NY)
        go(copy(wqh.at[:, pl.ds(pl.multiple_of(i * PAIR, PAIR), PAIR)], wqr.at[y], wsend.at[d], wrecv.at[y], at_y(i)))

    ring_out(0, 0)
    loads[4].wait()
    rq[...] = sum3(dot(q3, res[...], NN)).reshape(NC, HALF, ROWS)
    r_ex = go(copy(rq.at[1 - c], rqin, esend.at[2], erecv.at[1], sibling))
    wqr[y] = wqh[:, pl.ds(pl.multiple_of(y * PAIR, PAIR), PAIR)]
    for d in range(1, NY):
        i = other(y, d, NY)
        copy(wqr.at[i], wqr.at[i], wsend.at[d], wrecv.at[i], sibling).wait_recv()
    ring_out(0, 1)
    w_tok = wqr[0]
    for i in range(1, NY):
        w_tok = w_tok + wqr[i]
    sib_slot = gbuf.at[y * NC + (1 - c)]
    copy(sib_slot, sib_slot, esend.at[1], cown, sibling).wait_recv()
    pair = gbuf[pl.ds(y * NC, NC)].reshape(PAIR, ROWS)
    p_tok = sum3(dot(split3(w_tok), pair, NN))
    r_ex.wait_recv()
    ph[...] = p_tok + (rq[c] + rqin[...])

    for i in range(NX):
        for k in range(NZ):
            ps[i * NZ + k] = ph[ZR * k : ZR * (k + 1), XL * i : XL * (i + 1)]
    pl.semaphore_wait(plane, NZ - 1)
    for n, (dx, dz) in enumerate(FAR_PLANE):
        i = offset(dx, dz)
        go(copy(ps.at[i], pr.at[dp], psend.at[n], precv.at[dp], at_dp(i)))
    ring_in(1, 0)
    ring_out(1, 0)
    grad((0,), ())
    pr[dp] = ps[dp]
    for dx, dz in FAR_PLANE[::-1]:
        i = offset(dx, dz)
        copy(pr.at[i], pr.at[i], psend.at[0], precv.at[i], sibling).wait_recv()
    yr[y] = jnp.sum(pr[...], axis=0)
    for d in FAR_Y:
        i = other(y, d, NY)
        go(copy(yr.at[y], yr.at[y], ysend.at[d], yrecv.at[y], at_y(i)))
    ring_in(1, 1)
    ring_sibling(1)
    grad((1,), (1,))
    for d in range(1, NY):
        i = other(y, d, NY)
        copy(yr.at[i], yr.at[i], ysend.at[d], yrecv.at[i], sibling).wait_recv()
    pg[dp] = jnp.sum(yr[...], axis=0)
    for n, (dx, dz) in enumerate(FAR_PLANE):
        i = offset(dx, dz)
        go(copy(pg.at[dp], pg.at[dp], pgsend.at[n], pgrecv.at[dp], at_dp(i)))
    ring_out(1, 1)
    ring_in(2, 0)
    ring_out(2, 0)
    for dx, dz in FAR_PLANE[::-1]:
        i = offset(dx, dz)
        copy(pg.at[i], pg.at[i], pgsend.at[0], pgrecv.at[i], sibling).wait_recv()
    for i in range(NX):
        for k in range(NZ):
            pt[c, ZR * k : ZR * (k + 1), XL * i : XL * (i + 1)] = pg[i * NZ + k]
    go(copy(pt.at[c], pt.at[c], esend.at[3], erecv.at[2], sibling))
    copy(pt.at[1 - c], pt.at[1 - c], esend.at[3], erecv.at[2], sibling).wait_recv()

    p = pt[...].reshape(RANK, ROWS)
    p3 = split3(p)

    def chip_lanes(i):
        return pl.ds(pl.multiple_of(i * PAIR, PAIR), PAIR)

    def tokens_p(i):
        ubuf[:, chip_lanes(i)] = sum3(dot(p3, gbuf[pl.ds(i * NC, NC)].reshape(PAIR, ROWS), NT))

    tokens_p(y)
    own_u = ubuf.at[:, chip_lanes(y)]
    for d in FAR_U:
        go(copy(own_u, own_u, usend.at[d], urecv.at[d], at_y(other(y, d, NY))))
    qb[...] = jnp.zeros_like(qb)
    qb[:, :COLS] = sum3(dot(p3, res[...], NT))
    tokens_p(other(y, 1, NY))
    tokens_p(other(y, NY - 1, NY))
    ring_in(2, 1)
    ring_out(2, 1)
    ring_sibling(2)
    tokens_p(other(y, 2, NY))
    tokens_p(other(y, NY - 2, NY))
    for d in FAR_U:
        theirs = ubuf.at[:, chip_lanes(other(y, NY - d, NY))]
        copy(theirs, theirs, usend.at[d], urecv.at[d], sibling).wait_recv()
    qb[:, :COLS] += sum3(dot(split3(ubuf[...]), wbuf[...], NT))
    for d in FAR_X:
        i = other(x, d, NX)
        go(copy(qb.at[pl.ds(pl.multiple_of(i * QR, QR), QR)], qxr.at[x], qxsend.at[d], qxrecv.at[x], at_x(i)))

    ring_in(3, 0)
    ring_out(3, 0)
    inv[...] = inverse_factor(dot_exact(p, p, NT))
    qxr[x] = qb[pl.ds(pl.multiple_of(x * QR, QR), QR), :]
    for d in range(1, NX):
        i = other(x, d, NX)
        copy(qxr.at[i], qxr.at[i], qxsend.at[d], qxrecv.at[i], sibling).wait_recv()
    ring_in(3, 1)
    ring_out(3, 1)
    total = qxr[0]
    for i in range(1, NX):
        total = total + qxr[i]
    qzr[z] = total
    for d in FAR_Z:
        i = other(z, d, NZ)
        go(copy(qzr.at[z], qzr.at[z], qzsend.at[d], qzrecv.at[z], at_z(i)))
    grad((2,), (2,))
    ring_sibling(3)
    grad((3,), (3,))
    for d in range(1, NZ):
        i = other(z, d, NZ)
        copy(qzr.at[i], qzr.at[i], qzsend.at[d], qzrecv.at[i], sibling).wait_recv()
    total = qzr[0]
    for i in range(1, NZ):
        total = total + qzr[i]
    qt[x] = total
    for d in FAR_X:
        i = other(x, d, NX)
        go(copy(qt.at[x], qt.at[x], qgsend.at[d], qgrecv.at[x], at_x(i)))
    phat_ref[...] = dot_exact(inv[...], p, NN)
    ring_in(4, 0)
    ring_in(4, 1)
    ring_sibling(4)
    grad((), (4,))
    for d in range(1, NX):
        i = other(x, d, NX)
        copy(qt.at[i], qt.at[i], qgsend.at[d], qgrecv.at[i], sibling).wait_recv()
    qnext_ref[...] = dot_exact(inv[...], qt[...].reshape(RANK, QL), NN)
    for cp in pending:
        cp.wait_send()


def chain(inputs, out_grads, counts, residual, q_start):
    dma = pltpu.SemaphoreType.DMA
    vmem = pltpu.VMEM
    return pl.pallas_call(
        chain_kernel,
        out_shape=(
            vmem((COLS, ROWS), F32),
            vmem((RANK, ROWS), F32),
            vmem((RANK, QL), F32),
        ),
        in_specs=[pl.BlockSpec(memory_space=pl.ANY)] * 5,
        out_specs=(
            pl.BlockSpec(memory_space=pltpu.VMEM),
            pl.BlockSpec(memory_space=pltpu.VMEM),
            pl.BlockSpec(memory_space=pltpu.VMEM),
        ),
        scratch_shapes=[
            vmem((NY * NC, BLOCK, ROWS), BF16),
            vmem((COLS, TOK), BF16),
            vmem((1, TOK), jnp.int32),
            vmem((COLS, ROWS), BF16),
            vmem((RANK, COLS), F32),
            vmem((COLS, TOK), BF16),
            vmem((NC, HALF, TOK), F32),
            vmem((HALF, TOK), F32),
            vmem((HALF, TOK), F32),
            vmem((NY, HALF, PAIR), F32),
            vmem((NC, HALF, ROWS), F32),
            vmem((HALF, ROWS), F32),
            vmem((HALF, ROWS), F32),
            vmem((NX * NZ, ZR, XL), F32),
            vmem((NX * NZ, ZR, XL), F32),
            vmem((NY, ZR, XL), F32),
            vmem((NX * NZ, ZR, XL), F32),
            vmem((NC, HALF, ROWS), F32),
            vmem((RANK, QL), F32),
            vmem((NX, QR, QL), F32),
            vmem((NZ, QR, QL), F32),
            vmem((NX, QR, QL), F32),
            vmem((RANK, RANK), F32),
            vmem((RANK, TOK), F32),
            dma((5,)),
            dma((2, 4, 2)), dma((2, 4, 2)),
            dma((2, 4, 2)), dma((2, 4, 2)),
            dma,
            dma((4,)), dma((3,)),
            dma((NY,)), dma((NY,)),
            dma((NX * NZ,)), dma((NX * NZ,)),
            dma((NY,)), dma((NY,)),
            dma((NX * NZ,)), dma((NX * NZ,)),
            pltpu.SemaphoreType.REGULAR,
            dma((NX,)), dma((NX,)),
            dma((NZ,)), dma((NZ,)),
            dma((NX,)), dma((NX,)),
            dma((NY,)), dma((NY,)),
        ],
        compiler_params=pltpu.CompilerParams(
            collective_id=0, has_side_effects=True, vmem_limit_bytes=40 << 20
        ),
        name="chain",
    )(*(pltpu.with_memory_space_constraint(a, pltpu.HBM) for a in (inputs, out_grads, counts, residual, q_start)))


FINAL_LANES = 640
OWN = ROWS // (NX * NZ)


def final_kernel(
    merged_ref, phat_ref, qnext_ref, update_hbm, res_hbm, q_hbm,
    update, res, q, turned, sems,
):
    def high_low(v):
        high = v.astype(BF16)
        return high, (v - high.astype(F32)).astype(BF16)

    stores = []

    def store(src, dst):
        stores.append(pltpu.make_async_copy(src, dst, sems.at[len(stores)]))
        stores[-1].start()

    q[...] = qnext_ref[:, :COLS]
    store(q, q_hbm)
    high, low = high_low(qnext_ref[...].T)
    q_cols = jnp.concatenate([high, low, high], axis=1)[:COLS]
    for i in range(ROWS // FINAL_LANES):
        at = slice(i * FINAL_LANES, (i + 1) * FINAL_LANES)
        high, low = high_low(phat_ref[:, at])
        block = dot(q_cols, jnp.concatenate([high, high, low], axis=0), NN)
        res[:, at] = (merged_ref[:, at] - block * (1.0 / (NX * NZ))).astype(BF16)
        store(res.at[:, at], res_hbm.at[:, at])
    first = lax.axis_index("dp") * OWN
    base = jnp.minimum(first // 128, ROWS // 128 - 2) * 128
    turned[...] = phat_ref[:, pl.ds(pl.multiple_of(base, 128), 256)].T
    high, low = high_low(turned[pl.ds(pl.multiple_of(first - base, 8), OWN), :])
    update[...] = dot(jnp.concatenate([high, high, low], axis=1), q_cols, NT).astype(BF16)
    store(update, update_hbm)
    for cp in stores:
        cp.wait()


def final(merged, phat, qnext):
    shapes = ((OWN, COLS), BF16), ((COLS, ROWS), BF16), ((RANK, COLS), F32)
    return pl.pallas_call(
        final_kernel,
        out_shape=tuple(jax.ShapeDtypeStruct(*s) for s in shapes),
        in_specs=[pl.BlockSpec(memory_space=pltpu.VMEM)] * 3,
        out_specs=(pl.BlockSpec(memory_space=pl.ANY),) * 3,
        scratch_shapes=[
            *(pltpu.VMEM(*s) for s in shapes),
            pltpu.VMEM((256, RANK), F32),
            pltpu.SemaphoreType.DMA((ROWS // FINAL_LANES + 2,)),
        ],
        compiler_params=pltpu.CompilerParams(vmem_limit_bytes=24 << 20),
        name="final",
    )(*(pltpu.with_memory_space_constraint(a, pltpu.VMEM) for a in (merged, phat, qnext)))


def local(inputs, out_grads, counts, residual, q_start):
    merged, phat, qnext = chain(inputs[0], out_grads[0].T, counts, residual[0].T, q_start.T)
    update, residual_next, q_next = final(merged, phat, qnext)
    return update, residual_next.T[None], q_next.T


def solution(mesh):
    return jax.shard_map(
        local,
        mesh=mesh,
        in_specs=(
            P("dp", "mp", None),
            P("dp", None, "mp"),
            P("dp", None),
            P("dp", None, "mp"),
            P("mp", None),
        ),
        out_specs=(P("dp", "mp"), P("dp", None, "mp"), P("mp", None)),
        check_vma=False,
    )
```
